32 devices in a mesh: groups: 2 (over y), dp: 4 (over z), feat: 2 (over x), sub: 2 (over core).
Axes of the slice: x: 2, y: 2, z: 4, core: 2. Of those that a mesh axis runs over, the one named last changes fastest.
Arguments:
- layer_inputs: bfloat16 [14336, 4096], P(('groups', 'dp'), ('feat', 'sub')), parts along dimension 0, may hold values from -6 to 6
- output_grads: bfloat16 [14336, 4096], P(('groups', 'dp'), ('feat', 'sub')), parts along dimension 0, may hold values from -6 to 6
- proj_in: bfloat16 [4096, 64], P(('feat', 'sub')), may hold values from -0.09375 to 0.09375
- proj_out: bfloat16 [4096, 128], P(('feat', 'sub')), may hold values from -0.09375 to 0.09375
- lengths: int32 [8, 56], P(('groups', 'dp')), parts along dimension 0, may hold values from 1 to 128, 1792 in all within a row
- target_ids: int32 [512], P(('groups', 'dp')), parts along dimension 0, may hold values from 0 to 223
Outputs:
- covariance: float32 [16384, 8192], P(('groups', 'feat', 'sub'), 'dp'), parts along dimension 0
- scores: float32 [512, 224], P(('groups', 'dp'), ('feat', 'sub')), parts along dimension 0
The draws below stay inside these ranges and needn't reach their ends.
There are 2 independent parts, one for each index of `groups`. The reference program is written for one: setup_inputs(seed, part) draws one part's arguments, and reference() takes and returns one part's arrays. A program takes and returns all parts, laid end to end along the dimension named above; an argument that names none is the same for every part. Nothing has to cross between parts.
Inputs may be any that keep to these rules, and one draw needn't show every extreme that they name: Each row of lengths sums to 1792, its largest entry is exactly 128. `target_ids`: global sequence numbers.
All inputs are finite; a program needn't handle non-finite values.
Results may differ from the reference program's by a relative error of at most 0.004.
Values may be sent and summed in bfloat16 or wider, within the bound.
No kernel may reach another device: no remote copies, remote signals or barrier semaphores. Data moves between devices by JAX's collectives and lax.ppermute only.
A program may use at most 128 MiB of HBM per device.

```python
import math
import jax
import jax.numpy as jnp
import numpy as np
from jax import lax

D = 4096
R1 = 64
R2 = 128
MAXLEN = 128
TOK_DEV = 1792
SEQ_DEV = 56
TOKENS = 7168
SEQS = 224
NT = 256
N_DP = 4


def place_ends(entries, stream_key, smallest, high):
    extent = entries.shape
    place = [jax.random.randint(jax.random.fold_in(stream_key, axis), (), 0, extent[axis]) for axis in range(len(extent))]
    entries = entries.at[tuple(place)].set(smallest)
    longest = extent.index(max(extent))
    place[longest] = (place[longest] + 1) % extent[longest]
    return entries.at[tuple(place)].set(high)


def level_of(rng, extent, split, low, top_value):
    level = 1.0
    for axis_at, parts in split:
        heights = jax.random.uniform(jax.random.fold_in(jax.random.fold_in(rng, 6), axis_at), (parts,), jnp.float32, low / len(split), top_value / len(split))
        level = level * jnp.repeat(jnp.exp(heights), extent[axis_at] // parts).reshape((-1,) + (1,) * (len(extent) - 1 - axis_at))
    return level


def split_up(number_of, total, most, skew):
    portions = [(1 << 20) // math.isqrt(rank ** skew) + 1 for rank in range(2, number_of + 1)]
    surplus, counts = total - most - (number_of - 1), [1] * (number_of - 1)
    while surplus > 0:
        candidates = [i for i in range(number_of - 1) if counts[i] < most]
        mass, left = sum([portions[i] for i in candidates]), surplus
        for i in candidates:
            extra = min(most - counts[i], max(1, left * portions[i] // mass), surplus)
            counts[i] = counts[i] + extra
            surplus = surplus - extra
    return np.array([most] + counts)


def ragged_sizes(own_key, number_of, total, most, lean):
    if number_of == 2:
        one = jax.random.randint(own_key, (), max(1, total - most), min(most, total - 1) + 1)
        return jnp.stack([one, total - one])
    sizes = jnp.asarray(split_up(number_of, total, most, lean), jnp.int32)
    pairs = (number_of - 1) // 2
    source_of, receiver = sizes[1:1 + 2 * pairs:2], sizes[2:2 + 2 * pairs:2]
    slack = jnp.minimum(source_of - 1, most - receiver)
    moved = jax.random.randint(jax.random.fold_in(own_key, 1), (pairs,), 0, 1 << 20) % (slack + 1)
    sizes = sizes.at[1:1 + 2 * pairs:2].set(source_of - moved).at[2:2 + 2 * pairs:2].set(receiver + moved)
    return sizes[jax.random.permutation(jax.random.fold_in(own_key, 2), number_of)]


def bell_draw(stream_key, shape, scale, bound, pieces=(), kind=jnp.bfloat16):
    loudness = level_of(stream_key, shape, pieces, -0.22, 0.18) if pieces else 1.0
    entries = jax.random.normal(stream_key, shape, jnp.float32) * scale * loudness
    return jnp.minimum(jnp.maximum(entries, -bound), bound).astype(kind)


def setup_inputs(seed: int = 0, part: int = 0) -> dict:
    key_list = jax.random.split(jax.random.key(seed), 7)
    part_keys = jax.random.split(jax.random.fold_in(key_list[6], part), 7)
    return {
        "layer_inputs": bell_draw(part_keys[0], (TOKENS, D), 1.0, 6.0, ((0, 4), (1, 4))),
        "output_grads": bell_draw(part_keys[1], (TOKENS, D), 1.0, 6.0, ((0, 4), (1, 4))),
        "proj_in": bell_draw(key_list[2], (D, R1), D ** -0.5, 0.09375, ((0, 4),)),
        "proj_out": bell_draw(key_list[3], (D, R2), D ** -0.5, 0.09375, ((0, 4),)),
        "lengths": jax.vmap(lambda own: ragged_sizes(own, SEQ_DEV, TOK_DEV, MAXLEN, 2))(jax.random.split(part_keys[4], N_DP)).reshape((N_DP, SEQ_DEV)).astype(jnp.int32),
        "target_ids": place_ends(jax.random.randint(part_keys[5], (NT,), 0, SEQS), jax.random.fold_in(part_keys[5], 1), 0, SEQS - 1).astype(jnp.int32),
    }


def reference(layer_inputs, output_grads, proj_in, proj_out, lengths, target_ids):
    u_all = jnp.dot(layer_inputs, proj_in, preferred_element_type=jnp.float32)
    v_all = jnp.dot(output_grads, proj_out, preferred_element_type=jnp.float32)

    def block_features(items):
        u_block, v_block, len_block = items
        kron = (v_block[:, :, None] * u_block[:, None, :]).reshape(TOK_DEV, R2 * R1)
        len_block = len_block.astype(jnp.int32)
        ends = jnp.cumsum(len_block).astype(jnp.int32)
        starts = (ends - len_block).astype(jnp.int32)
        position = jnp.arange(TOK_DEV, dtype=jnp.int32)
        member = ((position[None, :] >= starts[:, None]) & (position[None, :] < ends[:, None])).astype(jnp.float32)
        member = member / jnp.sqrt(len_block.astype(jnp.float32))[:, None]
        summed = jnp.dot(member, kron, precision=lax.Precision.HIGHEST, preferred_element_type=jnp.float32)
        return summed.astype(jnp.bfloat16)
    features = lax.map(block_features, (u_all.reshape(N_DP, TOK_DEV, R1), v_all.reshape(N_DP, TOK_DEV, R2), lengths))
    features = features.reshape(SEQS, R1 * R2)
    covariance = jnp.dot(features.T, features, preferred_element_type=jnp.float32) / SEQS
    weights = 1.0 / (jnp.diagonal(covariance) + 1e-05)
    chosen = features[target_ids.astype(jnp.int32)]
    weighted = (chosen.astype(jnp.float32) * weights[None, :]).astype(jnp.bfloat16)
    scores = jnp.dot(weighted, features.T, preferred_element_type=jnp.float32) / jnp.sqrt(jnp.float32(R1 * R2))
    return (covariance, scores)
```

```python
import jax
import jax.numpy as jnp
from jax import lax
from jax.experimental import pallas as pl
from jax.experimental.pallas import tpu as pltpu
from jax.sharding import PartitionSpec as P

F32, BF16, I32 = jnp.float32, jnp.bfloat16, jnp.int32
WIDE = ("feat", "sub")
MIB = 1 << 20
VMEM = pl.BlockSpec(memory_space=pltpu.VMEM)
SMEM = pl.BlockSpec(memory_space=pltpu.SMEM)


def params(mib):
    return pltpu.CompilerParams(vmem_limit_bytes=mib * MIB)


def project_kernel(x_ref, g_ref, in_ref, out_ref, full_ref):
    rank_in = in_ref.shape[1]
    u = jnp.dot(x_ref[...], in_ref[...], preferred_element_type=F32)
    v = jnp.dot(g_ref[...], out_ref[...], preferred_element_type=F32)
    full_ref[0:rank_in, :] = jnp.transpose(u)
    full_ref[rank_in:, :] = jnp.transpose(v)


def project(layer_inputs, output_grads, proj_in, proj_out):
    rows, width = layer_inputs.shape
    tile = 256
    total = proj_in.shape[1] + proj_out.shape[1]
    return pl.pallas_call(
        project_kernel,
        grid=(rows // tile,),
        in_specs=[
            pl.BlockSpec((tile, width), lambda i: (i, 0)),
            pl.BlockSpec((tile, width), lambda i: (i, 0)),
            pl.BlockSpec(proj_in.shape, lambda i: (0, 0)),
            pl.BlockSpec(proj_out.shape, lambda i: (0, 0)),
        ],
        out_specs=pl.BlockSpec((total, tile), lambda i: (0, i)),
        out_shape=jax.ShapeDtypeStruct((total, rows), F32),
        compiler_params=params(16),
        name="project",
    )(layer_inputs, output_grads, proj_in, proj_out)


def split(x):
    high = x.astype(BF16)
    return high, (x - high.astype(F32)).astype(BF16)


def feature_kernel(start_ref, end_ref, u_ref, v_ref, scale_ref, feat_ref, uu, vh, vl, acc, wide):
    rank_in = u_ref.shape[0]
    share = v_ref.shape[0]
    tokens = u_ref.shape[1]
    seqs = scale_ref.shape[0]
    tile = 256
    high, low = split(u_ref[...])
    uu[0:rank_in, :] = high
    uu[rank_in:, :] = low
    high, low = split(v_ref[...])
    vh[...] = high
    vl[...] = low
    lane = lax.broadcasted_iota(I32, (8, tile), 1)
    left = lax.broadcasted_iota(I32, (8, 2 * rank_in), 1) < rank_in
    for group in range(seqs // 8):
        first = start_ref[8 * group]
        last = end_ref[8 * group + 7]
        acc[...] = jnp.zeros_like(acc)

        def step(k, carry):
            at = pl.multiple_of(k * tile, tile)
            tops, lows = [], []
            v_high = vh[:, pl.ds(at, tile)]
            v_low = vl[:, pl.ds(at, tile)]
            for s in range(8):
                begin = start_ref[8 * group + s] - at
                stop = end_ref[8 * group + s] - at
                inside = jnp.where((lane >= begin) & (lane < stop), 1.0, 0.0).astype(F32)
                inside = jnp.concatenate([inside] * (share // 8), axis=0).astype(BF16)
                tops.append(v_high * inside)
                lows.append(v_low * inside)
            right = uu[:, pl.ds(at, tile)]
            dims = (((1,), (1,)), ((), ()))
            total = lax.dot_general(jnp.concatenate(tops, 0), right, dims, preferred_element_type=F32)
            total += lax.dot_general(jnp.concatenate(lows, 0), right, dims, preferred_element_type=F32)
            acc[...] += total
            return carry

        lax.fori_loop(first // tile, (last + tile - 1) // tile, step, 0)
        factor = scale_ref[8 * group : 8 * group + 8, :]
        for pair in range(share // 2):
            even = acc[pl.ds(2 * pair, 8, stride=share), :]
            odd = acc[pl.ds(2 * pair + 1, 8, stride=share), :]
            even = even + pltpu.roll(even, rank_in, 1)
            odd = odd + pltpu.roll(odd, rank_in, 1)
            both = jnp.where(left, even, odd) * factor
            wide[8 * group : 8 * group + 8, 2 * rank_in * pair : 2 * rank_in * (pair + 1)] = both
    feat_ref[...] = wide[...].astype(BF16)


def features_of(starts, ends, u, v, scale):
    rank_in, tokens = u.shape
    share = v.shape[0]
    seqs = starts.shape[0]
    return pl.pallas_call(
        feature_kernel,
        in_specs=[SMEM, SMEM, VMEM, VMEM, VMEM],
        out_specs=VMEM,
        out_shape=jax.ShapeDtypeStruct((seqs, share * rank_in), BF16),
        scratch_shapes=[
            pltpu.VMEM((2 * rank_in, tokens), BF16),
            pltpu.VMEM((share, tokens), BF16),
            pltpu.VMEM((share, tokens), BF16),
            pltpu.VMEM((8 * share, 2 * rank_in), F32),
            pltpu.VMEM((seqs, share * rank_in), F32),
        ],
        compiler_params=params(16),
        name="features",
    )(starts, ends, u, v, scale)


def score_kernel(ids_ref, all_ref, part_ref):
    every = all_ref[...]
    seqs = every.shape[0]
    picks = ids_ref.shape[0]
    wide = every.astype(F32)
    diag = jnp.sum(wide * wide, axis=0, keepdims=True) / seqs
    weights = 1.0 / (diag + 1e-05)
    column = lax.broadcasted_iota(I32, (picks, seqs), 1)
    chosen_of = jnp.where(column == ids_ref[...], 1.0, 0.0).astype(BF16)
    chosen = jnp.dot(chosen_of, every, preferred_element_type=F32)
    weighted = (chosen * weights).astype(BF16)
    part_ref[...] = lax.dot_general(
        every, weighted, (((1,), (1,)), ((), ())), preferred_element_type=F32
    )


def partial_scores_of(ids, gathered):
    return pl.pallas_call(
        score_kernel,
        in_specs=[VMEM, VMEM],
        out_specs=VMEM,
        out_shape=jax.ShapeDtypeStruct((gathered.shape[0], ids.shape[0]), F32),
        compiler_params=params(24),
        name="partial_scores",
    )(ids[:, None], gathered)


def covariance_kernel(row_ref, col_ref, tile_ref):
    seqs = row_ref.shape[0]
    product = lax.dot_general(
        row_ref[...], col_ref[...], (((0,), (0,)), ((), ())), preferred_element_type=F32
    )
    tile_ref[...] = product * (1.0 / seqs)


def covariance_of(gathered, other_cols):
    seqs, rows = gathered.shape
    cols = other_cols.shape[1]
    tile = 256
    return pl.pallas_call(
        covariance_kernel,
        grid=(rows // tile,),
        in_specs=[
            pl.BlockSpec((seqs, tile), lambda i: (0, i)),
            pl.BlockSpec((seqs, cols), lambda i: (0, 0)),
        ],
        out_specs=pl.BlockSpec((tile, cols), lambda i: (i, 0)),
        out_shape=jax.ShapeDtypeStruct((rows, cols), F32),
        compiler_params=params(24),
        name="covariance",
    )(gathered, other_cols)


def both_ways(x, axis):
    return lax.ppermute(x, axis, [(0, 1), (1, 0)])


def reduced(partial, rank_in, share):
    feats, subs = lax.axis_size("feat"), lax.axis_size("sub")
    if feats != 2 or subs != 2:
        u = lax.psum(partial[:rank_in], WIDE)
        return u, lax.psum_scatter(partial[rank_in:], WIDE, scatter_dimension=0, tiled=True)
    feat, sub = lax.axis_index("feat"), lax.axis_index("sub")
    u = partial[:rank_in].reshape(2, rank_in // 2, -1)
    v = partial[rank_in:].reshape(2, 2, share, -1)
    keep = jnp.concatenate([jnp.where(sub == 0, u[0], u[1]), jnp.where(sub == 0, v[0, 0], v[0, 1]), jnp.where(sub == 0, v[1, 0], v[1, 1])])
    give = jnp.concatenate([jnp.where(sub == 0, u[1], u[0]), jnp.where(sub == 0, v[0, 1], v[0, 0]), jnp.where(sub == 0, v[1, 1], v[1, 0])])
    chip = keep + both_ways(give, "sub")
    half = rank_in // 2
    u_chip, v_low, v_high = chip[:half], chip[half : half + share], chip[half + share :]
    keep = jnp.concatenate([u_chip, jnp.where(feat == 0, v_low, v_high)])
    give = jnp.concatenate([u_chip, jnp.where(feat == 0, v_high, v_low)])
    whole = keep + both_ways(give, "feat")
    u_mine, v_mine = whole[:half], whole[half:]
    u_other = both_ways(u_mine, "sub")
    u = jnp.concatenate([jnp.where(sub == 0, u_mine, u_other), jnp.where(sub == 0, u_other, u_mine)])
    return u, v_mine


def column_block(gathered, col_width):
    group = lax.axis_size(WIDE)
    block_width = gathered.shape[1]
    dp = lax.axis_size("dp")
    at = lax.axis_index("dp")
    if lax.axis_size("feat") == 2 and lax.axis_size("sub") == 2 and dp == 4:
        axes = ("dp",) + WIDE
        me = lax.axis_index(WIDE)
        over = lax.ppermute(gathered, axes, [(4 * d + d, 4 * d + (d ^ 2)) for d in range(4)])
        held = jnp.where(me == at, gathered, over)
        across = [(4 * d + d, 4 * d + (d ^ 1)) for d in range(4)]
        across += [(4 * d + (d ^ 2), 4 * d + (d ^ 3)) for d in range(4)]
        beside = lax.ppermute(held, axes, across)
        return jnp.where((me == at) | (me == (at ^ 2)), held, beside)
    col_start = at * col_width
    owner = col_start // block_width
    own_slice = lax.dynamic_slice_in_dim(gathered, col_start % block_width, col_width, 1)
    every_slice = lax.all_gather(own_slice, WIDE, axis=1, tiled=True)
    return lax.dynamic_slice_in_dim(every_slice, owner * col_width, col_width, 1)


def shards(layer_inputs, output_grads, proj_in, proj_out, lengths, target_ids):
    group = lax.axis_size(WIDE)
    rank_in = proj_in.shape[1]
    share = proj_out.shape[1] // group
    partial = project(layer_inputs, output_grads, proj_in, proj_out)
    u, v_mine = reduced(partial, rank_in, share)
    seq_len = lengths[0]
    ends = jnp.cumsum(seq_len)
    starts = ends - seq_len
    scale = jnp.broadcast_to(1.0 / jnp.sqrt(seq_len.astype(F32))[:, None], (seq_len.shape[0], 2 * rank_in))
    local_feat = features_of(starts, ends, u, v_mine, scale)
    gathered = lax.all_gather(local_feat, "dp", axis=0, tiled=True)
    block_width = gathered.shape[1]
    col_width = block_width * group // lax.axis_size("dp")
    other_cols = column_block(gathered, col_width)
    part = partial_scores_of(target_ids, gathered)
    own = part.shape[0] // group
    me = lax.axis_index(WIDE)
    if lax.axis_size("feat") == 2 and lax.axis_size("sub") == 2:
        pieces = part.reshape(group, own, -1)
        total = lax.dynamic_index_in_dim(pieces, me, 0, keepdims=False)
        for k in range(1, group):
            given = lax.dynamic_index_in_dim(pieces, me ^ k, 0, keepdims=False)
            total = total + lax.ppermute(given, WIDE, [(i, i ^ k) for i in range(group)])
    else:
        total = lax.psum_scatter(part, WIDE, scatter_dimension=0, tiled=True)
    scores = jnp.transpose(total) / jnp.sqrt(jnp.float32(block_width * group))
    return (covariance_of(gathered, other_cols), scores)


def solution(mesh):
    placed = (
        P(("groups", "dp"), ("feat", "sub")),
        P(("groups", "dp"), ("feat", "sub")),
        P(("feat", "sub"), None),
        P(("feat", "sub"), None),
        P(("groups", "dp"), None),
        P(("groups", "dp")),
    )
    return jax.shard_map(
        shards,
        mesh=mesh,
        in_specs=placed,
        out_specs=(P(("groups", "feat", "sub"), "dp"), P(("groups", "dp"), ("feat", "sub"))),
        check_vma=False,
    )
```

```python
import jax
import jax.numpy as jnp
from jax import lax
from jax.experimental import pallas as pl
from jax.experimental.pallas import tpu as pltpu
from jax.sharding import PartitionSpec as P

F32, BF16, I32 = jnp.float32, jnp.bfloat16, jnp.int32
WIDE = ("feat", "sub")
MIB = 1 << 20
VMEM = pl.BlockSpec(memory_space=pltpu.VMEM)
SMEM = pl.BlockSpec(memory_space=pltpu.SMEM)


def params(mib):
    return pltpu.CompilerParams(vmem_limit_bytes=mib * MIB)


def project_kernel(x_hbm, g_hbm, in_ref, out_ref, full_ref, x_ref, g_ref, flip_ref, x_sem, g_sem):
    rank_in = in_ref.shape[0]
    rows = x_ref.shape[0]
    steps = x_sem.shape[0]
    tile = rows // steps
    copies = []
    for i in range(steps):
        at = pl.ds(i * tile, tile)
        copies.append(
            (
                pltpu.make_async_copy(x_hbm.at[at], x_ref.at[at], x_sem.at[i]),
                pltpu.make_async_copy(g_hbm.at[at], g_ref.at[at], g_sem.at[i]),
            )
        )
    for x_copy, g_copy in copies:
        x_copy.start()
        g_copy.start()
    flip_ref[...] = jnp.transpose(in_ref[...])
    for i, (x_copy, g_copy) in enumerate(copies):
        at = slice(i * tile, (i + 1) * tile)
        x_copy.wait()
        u = jnp.dot(x_ref[at, :], flip_ref[...], preferred_element_type=F32)
        full_ref[0:rank_in, at] = jnp.transpose(u)
        g_copy.wait()
        v = jnp.dot(g_ref[at, :], out_ref[...], preferred_element_type=F32)
        full_ref[rank_in:, at] = jnp.transpose(v)


def project(layer_inputs, output_grads, proj_in, proj_out):
    rows, width = layer_inputs.shape
    steps = rows // 256
    total = proj_in.shape[1] + proj_out.shape[1]
    return pl.pallas_call(
        project_kernel,
        in_specs=[pl.BlockSpec(memory_space=pltpu.HBM)] * 2 + [VMEM, VMEM],
        out_specs=VMEM,
        out_shape=jax.ShapeDtypeStruct((total, rows), F32),
        scratch_shapes=[
            pltpu.VMEM((rows, width), BF16),
            pltpu.VMEM((rows, width), BF16),
            pltpu.VMEM(proj_in.shape, BF16),
            pltpu.SemaphoreType.DMA((steps,)),
            pltpu.SemaphoreType.DMA((steps,)),
        ],
        compiler_params=params(58),
        name="project",
    )(layer_inputs, output_grads, jnp.transpose(proj_in), proj_out)


def split(x):
    high = x.astype(BF16)
    return high, (x - high.astype(F32)).astype(BF16)


def feature_kernel(start_ref, end_ref, u_ref, v_ref, scale_ref, feat_ref, uu, vh, vl, acc, wide):
    rank_in = u_ref.shape[0]
    share = v_ref.shape[0]
    tokens = u_ref.shape[1]
    seqs = scale_ref.shape[0]
    tile = 256
    high, low = split(u_ref[...])
    uu[0:rank_in, :] = high
    uu[rank_in:, :] = low
    high, low = split(v_ref[...])
    vh[...] = high
    vl[...] = low
    lane = lax.broadcasted_iota(I32, (8, tile), 1)
    left = lax.broadcasted_iota(I32, (8, 2 * rank_in), 1) < rank_in
    for group in range(seqs // 8):
        first = start_ref[8 * group]
        last = end_ref[8 * group + 7]
        acc[...] = jnp.zeros_like(acc)

        def step(k, carry):
            at = pl.multiple_of(k * tile, tile)
            tops, lows = [], []
            v_high = vh[:, pl.ds(at, tile)]
            v_low = vl[:, pl.ds(at, tile)]
            for s in range(8):
                begin = start_ref[8 * group + s] - at
                stop = end_ref[8 * group + s] - at
                inside = jnp.where((lane >= begin) & (lane < stop), 1.0, 0.0).astype(F32)
                inside = jnp.concatenate([inside] * (share // 8), axis=0).astype(BF16)
                tops.append(v_high * inside)
                lows.append(v_low * inside)
            right = uu[:, pl.ds(at, tile)]
            dims = (((1,), (1,)), ((), ()))
            total = lax.dot_general(jnp.concatenate(tops, 0), right, dims, preferred_element_type=F32)
            total += lax.dot_general(jnp.concatenate(lows, 0), right, dims, preferred_element_type=F32)
            acc[...] += total
            return carry

        lax.fori_loop(first // tile, (last + tile - 1) // tile, step, 0)
        factor = scale_ref[8 * group : 8 * group + 8, :]
        for pair in range(share // 2):
            even = acc[pl.ds(2 * pair, 8, stride=share), :]
            odd = acc[pl.ds(2 * pair + 1, 8, stride=share), :]
            even = even + pltpu.roll(even, rank_in, 1)
            odd = odd + pltpu.roll(odd, rank_in, 1)
            both = jnp.where(left, even, odd) * factor
            wide[8 * group : 8 * group + 8, 2 * rank_in * pair : 2 * rank_in * (pair + 1)] = both
    feat_ref[...] = wide[...].astype(BF16)


def features_of(starts, ends, u, v, scale):
    rank_in, tokens = u.shape
    share = v.shape[0]
    seqs = starts.shape[0]
    return pl.pallas_call(
        feature_kernel,
        in_specs=[SMEM, SMEM, VMEM, VMEM, VMEM],
        out_specs=VMEM,
        out_shape=jax.ShapeDtypeStruct((seqs, share * rank_in), BF16),
        scratch_shapes=[
            pltpu.VMEM((2 * rank_in, tokens), BF16),
            pltpu.VMEM((share, tokens), BF16),
            pltpu.VMEM((share, tokens), BF16),
            pltpu.VMEM((8 * share, 2 * rank_in), F32),
            pltpu.VMEM((seqs, share * rank_in), F32),
        ],
        compiler_params=params(16),
        name="features",
    )(starts, ends, u, v, scale)


def score_kernel(ids_ref, all_ref, part_ref):
    every = all_ref[...]
    seqs = every.shape[0]
    picks = ids_ref.shape[0]
    wide = every.astype(F32)
    diag = jnp.sum(wide * wide, axis=0, keepdims=True) / seqs
    weights = 1.0 / (diag + 1e-05)
    column = lax.broadcasted_iota(I32, (picks, seqs), 1)
    chosen_of = jnp.where(column == ids_ref[...], 1.0, 0.0).astype(BF16)
    chosen = jnp.dot(chosen_of, every, preferred_element_type=F32)
    weighted = (chosen * weights).astype(BF16)
    part_ref[...] = lax.dot_general(
        every, weighted, (((1,), (1,)), ((), ())), preferred_element_type=F32
    )


def partial_scores_of(ids, gathered):
    return pl.pallas_call(
        score_kernel,
        in_specs=[VMEM, VMEM],
        out_specs=VMEM,
        out_shape=jax.ShapeDtypeStruct((gathered.shape[0], ids.shape[0]), F32),
        compiler_params=params(24),
        cost_estimate=pl.CostEstimate(flops=8 * gathered.size * ids.shape[0], bytes_accessed=2 * gathered.size, transcendentals=0),
        name="partial_scores",
    )(ids[:, None], gathered)


def covariance_kernel(row_ref, col_ref, tile_ref):
    seqs = row_ref.shape[0]
    product = lax.dot_general(
        row_ref[...], col_ref[...], (((0,), (0,)), ((), ())), preferred_element_type=F32
    )
    tile_ref[...] = product * (1.0 / seqs)


def covariance_of(gathered, other_cols):
    seqs, rows = gathered.shape
    cols = other_cols.shape[1]
    tile = 256
    return pl.pallas_call(
        covariance_kernel,
        grid=(rows // tile,),
        in_specs=[
            pl.BlockSpec((seqs, tile), lambda i: (0, i)),
            pl.BlockSpec((seqs, cols), lambda i: (0, 0)),
        ],
        out_specs=pl.BlockSpec((tile, cols), lambda i: (i, 0)),
        out_shape=jax.ShapeDtypeStruct((rows, cols), F32),
        compiler_params=params(24),
        cost_estimate=pl.CostEstimate(flops=2 * seqs * rows * cols, bytes_accessed=4 * rows * cols, transcendentals=0),
        name="covariance",
    )(gathered, other_cols)


def both_ways(x, axis):
    return lax.ppermute(x, axis, [(0, 1), (1, 0)])


def reduced(partial, rank_in, share):
    feats, subs = lax.axis_size("feat"), lax.axis_size("sub")
    if feats != 2 or subs != 2:
        u = lax.psum(partial[:rank_in], WIDE)
        return u, lax.psum_scatter(partial[rank_in:], WIDE, scatter_dimension=0, tiled=True)
    feat, sub = lax.axis_index("feat"), lax.axis_index("sub")
    u = partial[:rank_in].reshape(2, rank_in // 2, -1)
    v = partial[rank_in:].reshape(2, 2, share, -1)
    keep = jnp.concatenate([jnp.where(sub == 0, u[0], u[1]), jnp.where(sub == 0, v[0, 0], v[0, 1]), jnp.where(sub == 0, v[1, 0], v[1, 1])])
    give = jnp.concatenate([jnp.where(sub == 0, u[1], u[0]), jnp.where(sub == 0, v[0, 1], v[0, 0]), jnp.where(sub == 0, v[1, 1], v[1, 0])])
    chip = keep + both_ways(give, "sub")
    half = rank_in // 2
    u_chip, v_low, v_high = chip[:half], chip[half : half + share], chip[half + share :]
    keep = jnp.concatenate([u_chip, jnp.where(feat == 0, v_low, v_high)])
    give = jnp.concatenate([u_chip, jnp.where(feat == 0, v_high, v_low)])
    whole = keep + both_ways(give, "feat")
    u_mine, v_mine = whole[:half], whole[half:]
    u_other = both_ways(u_mine, "sub")
    u = jnp.concatenate([jnp.where(sub == 0, u_mine, u_other), jnp.where(sub == 0, u_other, u_mine)])
    return u, v_mine


def is_square():
    return lax.axis_size("feat") == 2 and lax.axis_size("sub") == 2 and lax.axis_size("dp") == 4


RING = (0, 1, 3, 2)


def ring_place(d):
    return d ^ (d >> 1)


def around(part):
    return lax.ppermute(part, "dp", [(RING[i], RING[(i + 1) % 4]) for i in range(4)])


def sent_across(part):
    return lax.ppermute(part, ("dp",) + WIDE, [(4 * d + d, 4 * d + (d ^ 2)) for d in range(4)])


def spread(part, over):
    at = lax.axis_index("dp")
    me = lax.axis_index(WIDE)
    held = jnp.where(me == at, part, over)
    pairs = [(4 * d + d, 4 * d + (d ^ 1)) for d in range(4)]
    pairs += [(4 * d + (d ^ 2), 4 * d + (d ^ 3)) for d in range(4)]
    beside = lax.ppermute(held, ("dp",) + WIDE, pairs)
    return jnp.where((me == at) | (me == (at ^ 2)), held, beside)


def column_block(gathered, col_width):
    block_width = gathered.shape[1]
    col_start = lax.axis_index("dp") * col_width
    owner = col_start // block_width
    own_slice = lax.dynamic_slice_in_dim(gathered, col_start % block_width, col_width, 1)
    every_slice = lax.all_gather(own_slice, WIDE, axis=1, tiled=True)
    return lax.dynamic_slice_in_dim(every_slice, owner * col_width, col_width, 1)


def shards(layer_inputs, output_grads, proj_in, proj_out, lengths, target_ids):
    group = lax.axis_size(WIDE)
    rank_in = proj_in.shape[1]
    share = proj_out.shape[1] // group
    partial = project(layer_inputs, output_grads, proj_in, proj_out)
    u, v_mine = reduced(partial, rank_in, share)
    seq_len = lengths[0]
    ends = jnp.cumsum(seq_len)
    starts = ends - seq_len
    scale = jnp.broadcast_to(1.0 / jnp.sqrt(seq_len.astype(F32))[:, None], (seq_len.shape[0], 2 * rank_in))
    local_feat = features_of(starts, ends, u, v_mine, scale)
    me = lax.axis_index(WIDE)
    at = lax.axis_index("dp")
    if is_square():
        chunks, across = [local_feat], []
        for k in range(4):
            if k < 3:
                chunks.append(around(chunks[k]))
            across.append(sent_across(chunks[k]))
            if k < 3:
                chunks[-1], across[-1] = lax.optimization_barrier((chunks[-1], across[-1]))
        gathered = jnp.concatenate(chunks)
        early = spread(jnp.concatenate(chunks[:3]), jnp.concatenate(across[:3]))
        other_cols = jnp.concatenate([early, spread(chunks[3], across[3])])
        seqs = local_feat.shape[0]
        ids = ((ring_place(at) - ring_place(target_ids // seqs)) & 3) * seqs + target_ids % seqs
    else:
        gathered = lax.all_gather(local_feat, "dp", axis=0, tiled=True)
        other_cols = column_block(gathered, gathered.shape[1] * group // lax.axis_size("dp"))
        ids = target_ids
    part = partial_scores_of(ids, gathered)
    own = part.shape[0] // group
    if is_square():
        pieces = part.reshape(group, own, -1)
        total = lax.dynamic_index_in_dim(pieces, (ring_place(at) - ring_place(me)) & 3, 0, keepdims=False)
        for k in range(1, group):
            given = lax.dynamic_index_in_dim(pieces, (ring_place(at) - ring_place(me ^ k)) & 3, 0, keepdims=False)
            total = total + lax.ppermute(given, WIDE, [(i, i ^ k) for i in range(group)])
    else:
        total = lax.psum_scatter(part, WIDE, scatter_dimension=0, tiled=True)
    scores = jnp.transpose(total) / jnp.sqrt(jnp.float32(gathered.shape[1] * group))
    return (covariance_of(gathered, other_cols), scores)


def solution(mesh):
    placed = (
        P(("groups", "dp"), ("feat", "sub")),
        P(("groups", "dp"), ("feat", "sub")),
        P(("feat", "sub"), None),
        P(("feat", "sub"), None),
        P(("groups", "dp"), None),
        P(("groups", "dp")),
    )
    return jax.shard_map(
        shards,
        mesh=mesh,
        in_specs=placed,
        out_specs=(P(("groups", "feat", "sub"), "dp"), P(("groups", "dp"), ("feat", "sub"))),
        check_vma=False,
    )
```

```python
import jax
import jax.numpy as jnp
from jax import lax
from jax.experimental import pallas as pl
from jax.experimental.pallas import tpu as pltpu
from jax.sharding import PartitionSpec as P

F32, BF16, I32 = jnp.float32, jnp.bfloat16, jnp.int32
WIDE = ("feat", "sub")
MIB = 1 << 20
VMEM = pl.BlockSpec(memory_space=pltpu.VMEM)
SMEM = pl.BlockSpec(memory_space=pltpu.SMEM)


def params(mib):
    return pltpu.CompilerParams(vmem_limit_bytes=mib * MIB)


def project_kernel(x_ref, weight_ref, full_ref):
    tile = 256
    for i in range(x_ref.shape[0] // tile):
        at = slice(i * tile, (i + 1) * tile)
        product = jnp.dot(x_ref[at, :], weight_ref[...], preferred_element_type=F32)
        full_ref[:, at] = jnp.transpose(product)


def project_flipped_kernel(x_ref, weight_ref, full_ref, flip_ref):
    flip_ref[...] = jnp.transpose(weight_ref[...])
    project_kernel(x_ref, flip_ref, full_ref)


def project(x, weight, flipped):
    rows, width = x.shape
    rank = weight.shape[0] if flipped else weight.shape[1]
    return pl.pallas_call(
        project_flipped_kernel if flipped else project_kernel,
        in_specs=[VMEM, VMEM],
        out_specs=VMEM,
        out_shape=jax.ShapeDtypeStruct((rank, rows), F32),
        scratch_shapes=[pltpu.VMEM((width, rank), BF16)] if flipped else [],
        compiler_params=params(16),
        cost_estimate=pl.CostEstimate(
            flops=(40 if flipped else 2) * rows * width * rank, bytes_accessed=2 * x.size, transcendentals=0
        ),
        name="project",
    )(x, weight)


def split(x):
    high = x.astype(BF16)
    return high, (x - high.astype(F32)).astype(BF16)


def feature_kernel(start_ref, end_ref, u_ref, v_ref, scale_ref, feat_ref, uu, vh, vl, acc, wide):
    rank_in = u_ref.shape[0]
    share = v_ref.shape[0]
    tokens = u_ref.shape[1]
    seqs = scale_ref.shape[0]
    tile = 256
    high, low = split(u_ref[...])
    uu[:tokens, :] = jnp.transpose(jnp.concatenate([high, low], axis=0))
    uu[tokens:, :] = jnp.zeros((uu.shape[0] - tokens, uu.shape[1]), BF16)
    high, low = split(v_ref[...])
    vh[:, :tokens] = high
    vl[:, :tokens] = low
    for ref in (vh, vl):
        ref[:, tokens:] = jnp.zeros((ref.shape[0], ref.shape[1] - tokens), BF16)
    lane = lax.broadcasted_iota(I32, (8, tile), 1)
    left = lax.broadcasted_iota(I32, (8, 2 * rank_in), 1) < rank_in
    for group in range(seqs // 8):
        sets = (8 * group, 8 * group + 4)
        bases = [(start_ref[s] // 128) * 128 for s in sets]
        needs = [(end_ref[s + 3] - base + tile - 1) // tile for s, base in zip(sets, bases)]
        acc[...] = jnp.zeros_like(acc)

        def step(k, carry):
            for i in range(2):
                at = pl.multiple_of(bases[i] + k * tile, 128)
                tops, lows = [], []
                v_high = vh[:, pl.ds(at, tile)]
                v_low = vl[:, pl.ds(at, tile)]
                for s in range(sets[i], sets[i] + 4):
                    begin = start_ref[s] - at
                    stop = end_ref[s] - at
                    inside = jnp.where((lane >= begin) & (lane < stop), 1.0, 0.0).astype(F32)
                    inside = jnp.concatenate([inside] * (share // 8), axis=0).astype(BF16)
                    tops.append(v_high * inside)
                    lows.append(v_low * inside)
                total = jnp.dot(
                    jnp.concatenate(tops + lows, 0),
                    uu[pl.ds(at, tile), :],
                    preferred_element_type=F32,
                )
                rows = slice(4 * share * i, 4 * share * (i + 1))
                acc[rows, :] += total[: 4 * share] + total[4 * share :]
            return carry

        lax.fori_loop(0, jnp.maximum(needs[0], needs[1]), step, 0)
        factor = scale_ref[8 * group : 8 * group + 8, :]
        for pair in range(share // 2):
            even = acc[pl.ds(2 * pair, 8, stride=share), :]
            odd = acc[pl.ds(2 * pair + 1, 8, stride=share), :]
            even = even + pltpu.roll(even, rank_in, 1)
            odd = odd + pltpu.roll(odd, rank_in, 1)
            both = jnp.where(left, even, odd) * factor
            wide[8 * group : 8 * group + 8, 2 * rank_in * pair : 2 * rank_in * (pair + 1)] = both
    feat_ref[...] = wide[...].astype(BF16)


def features_of(starts, ends, u, v, scale):
    rank_in, tokens = u.shape
    share = v.shape[0]
    seqs = starts.shape[0]
    return pl.pallas_call(
        feature_kernel,
        in_specs=[SMEM, SMEM, VMEM, VMEM, VMEM],
        out_specs=VMEM,
        out_shape=jax.ShapeDtypeStruct((seqs, share * rank_in), BF16),
        scratch_shapes=[
            pltpu.VMEM((tokens + 768, 2 * rank_in), BF16),
            pltpu.VMEM((share, tokens + 768), BF16),
            pltpu.VMEM((share, tokens + 768), BF16),
            pltpu.VMEM((8 * share, 2 * rank_in), F32),
            pltpu.VMEM((seqs, share * rank_in), F32),
        ],
        compiler_params=params(16),
        name="features",
    )(starts, ends, u, v, scale)


def score_kernel(ids_ref, all_ref, square_ref, part_ref):
    every = all_ref[...]
    seqs = every.shape[0]
    picks = ids_ref.shape[0]
    weights = 1.0 / (square_ref[...] / seqs + 1e-05)
    column = lax.broadcasted_iota(I32, (picks, seqs), 1)
    chosen_of = jnp.where(column == ids_ref[...], 1.0, 0.0).astype(BF16)
    chosen = jnp.dot(chosen_of, every, preferred_element_type=F32)
    weighted = (chosen * weights).astype(BF16)
    part_ref[...] = lax.dot_general(
        every, weighted, (((1,), (1,)), ((), ())), preferred_element_type=F32
    )


def partial_scores_of(ids, gathered, squares):
    return pl.pallas_call(
        score_kernel,
        in_specs=[VMEM, VMEM, VMEM],
        out_specs=VMEM,
        out_shape=jax.ShapeDtypeStruct((gathered.shape[0], ids.shape[0]), F32),
        compiler_params=params(24),
        cost_estimate=pl.CostEstimate(flops=8 * gathered.size * ids.shape[0], bytes_accessed=2 * gathered.size, transcendentals=0),
        name="partial_scores",
    )(ids[:, None], gathered, squares)


def covariance_kernel(row_ref, col_ref, tile_hbm, tile_ref, sem):
    seqs = row_ref.shape[0]
    steps = sem.shape[0]
    tile = tile_ref.shape[0] // steps
    copies = []
    for i in range(steps):
        at = slice(i * tile, (i + 1) * tile)
        product = lax.dot_general(
            row_ref[:, at], col_ref[...], (((0,), (0,)), ((), ())), preferred_element_type=F32
        )
        tile_ref[at, :] = product * (1.0 / seqs)
        rows = pl.ds(i * tile, tile)
        copies.append(pltpu.make_async_copy(tile_ref.at[rows], tile_hbm.at[rows], sem.at[i]))
        copies[-1].start()
    for copy in copies:
        copy.wait()


def covariance_of(gathered, other_cols):
    seqs, rows = gathered.shape
    cols = other_cols.shape[1]
    steps = rows // 256
    return pl.pallas_call(
        covariance_kernel,
        in_specs=[VMEM, VMEM],
        out_specs=pl.BlockSpec(memory_space=pltpu.HBM),
        out_shape=jax.ShapeDtypeStruct((rows, cols), F32),
        scratch_shapes=[pltpu.VMEM((rows, cols), F32), pltpu.SemaphoreType.DMA((steps,))],
        compiler_params=params(32),
        cost_estimate=pl.CostEstimate(flops=2 * seqs * rows * cols, bytes_accessed=4 * rows * cols, transcendentals=0),
        name="covariance",
    )(gathered, other_cols)


def both_ways(x, axis):
    return lax.ppermute(x, axis, [(0, 1), (1, 0)])


def picked(index, low, high):
    return jnp.where(index == 0, low, high)


STEPS = 32000.0


def exchanged(keep, give):
    top = jnp.max(jnp.abs(give), axis=1, keepdims=True)
    power = jnp.ceil(jnp.log2(jnp.maximum(top, 1e-30)))
    coded = jnp.round(give * (jnp.exp2(-power) * STEPS))
    sent = jnp.concatenate([coded, jnp.broadcast_to(power, (give.shape[0], 128))], axis=1)
    got = both_ways(sent.astype(jnp.int16), "feat").astype(F32)
    return keep + got[:, :-128] * (jnp.exp2(got[:, -128:-127]) * (1.0 / STEPS))


def u_of_chip(u):
    half = u.shape[0] // 2
    sub = lax.axis_index("sub")
    return picked(sub, u[:half], u[half:]) + both_ways(picked(sub, u[half:], u[:half]), "sub")


def reduced(u_chip, v, share):
    feat, sub = lax.axis_index("feat"), lax.axis_index("sub")
    u_mine = exchanged(u_chip, u_chip)
    u_other = both_ways(u_mine, "sub")
    u = jnp.concatenate([picked(sub, u_mine, u_other), picked(sub, u_other, u_mine)])
    v = v.reshape(2, 2, share, -1)
    v_chip = picked(sub, v[:, 0], v[:, 1]) + both_ways(picked(sub, v[:, 1], v[:, 0]), "sub")
    v_mine = exchanged(picked(feat, v_chip[0], v_chip[1]), picked(feat, v_chip[1], v_chip[0]))
    return u, v_mine


def is_square():
    return lax.axis_size("feat") == 2 and lax.axis_size("sub") == 2 and lax.axis_size("dp") == 4


RING = (0, 1, 3, 2)


def ring_place(d):
    return d ^ (d >> 1)


def around(part):
    return lax.ppermute(part, "dp", [(RING[i], RING[(i + 1) % 4]) for i in range(4)])


def on_owner_chip():
    return (lax.axis_index(WIDE) ^ lax.axis_index("dp")) < 2


def owned(part, other):
    return jnp.where(lax.axis_index(WIDE) == lax.axis_index("dp"), part, other)


def sent_across(part, axis):
    size = part.shape[axis] // 2
    low = lax.slice_in_dim(part, 0, size, axis=axis)
    high = lax.slice_in_dim(part, size, 2 * size, axis=axis)
    half = picked(lax.axis_index("sub"), low, high)
    return both_ways(half, "feat")


def spread(part, mine, other, axis):
    sub = lax.axis_index("sub")
    both = jnp.concatenate([picked(sub, mine, other), picked(sub, other, mine)], axis=axis)
    return jnp.where(on_owner_chip(), part, both)


def summed_squares(part):
    return jnp.sum(jnp.square(part.astype(F32)), axis=0, keepdims=True)


def column_block(gathered, col_width):
    block_width = gathered.shape[1]
    col_start = lax.axis_index("dp") * col_width
    owner = col_start // block_width
    own_slice = lax.dynamic_slice_in_dim(gathered, col_start % block_width, col_width, 1)
    every_slice = lax.all_gather(own_slice, WIDE, axis=1, tiled=True)
    return lax.dynamic_slice_in_dim(every_slice, owner * col_width, col_width, 1)


def shards(layer_inputs, output_grads, proj_in, proj_out, lengths, target_ids):
    group = lax.axis_size(WIDE)
    rank_in = proj_in.shape[1]
    share = proj_out.shape[1] // group
    u = project(layer_inputs, jnp.transpose(proj_in), True)
    if is_square():
        u_chip, proj_out = lax.optimization_barrier((u_of_chip(u), proj_out))
        v = project(output_grads, proj_out, False)
        u, v_mine = reduced(u_chip, v, share)
    else:
        v = project(output_grads, proj_out, False)
        u = lax.psum(u, WIDE)
        v_mine = lax.psum_scatter(v, WIDE, scatter_dimension=0, tiled=True)
    seq_len = lengths[0]
    ends = jnp.cumsum(seq_len)
    starts = ends - seq_len
    scale = jnp.broadcast_to(1.0 / jnp.sqrt(seq_len.astype(F32))[:, None], (seq_len.shape[0], 2 * rank_in))
    local_feat = features_of(starts, ends, u, v_mine, scale)
    me = lax.axis_index(WIDE)
    at = lax.axis_index("dp")
    if is_square():
        chunks = [local_feat]
        chunks.append(around(chunks[0]))
        chunks.append(around(chunks[1]))
        pair = jnp.concatenate(chunks[:2])
        pair = owned(pair, both_ways(pair, "sub"))
        pair_over = sent_across(pair, 0)
        chunks[2], pair_over = lax.optimization_barrier((chunks[2], pair_over))
        chunks.append(around(chunks[2]))
        third = owned(chunks[2], both_ways(chunks[2], "sub"))
        third_over = sent_across(third, 1)
        pair_other = both_ways(pair_over, "sub")
        chunks[3], third_over, pair_other = lax.optimization_barrier((chunks[3], third_over, pair_other))
        last = owned(chunks[3], both_ways(chunks[3], "sub"))
        third_other = both_ways(third_over, "sub")
        gathered = jnp.concatenate(chunks)
        squares = summed_squares(gathered)
        seqs = local_feat.shape[0]
        ids = ((ring_place(at) - ring_place(target_ids // seqs)) & 3) * seqs + target_ids % seqs
    else:
        gathered = lax.all_gather(local_feat, "dp", axis=0, tiled=True)
        other_cols = column_block(gathered, gathered.shape[1] * group // lax.axis_size("dp"))
        ids = target_ids
        squares = summed_squares(gathered)
    if is_square():
        last, ids = lax.optimization_barrier((last, ids))
        last_over = sent_across(last, 1)
    part = partial_scores_of(ids, gathered, squares)
    own = part.shape[0] // group
    if is_square():
        places = [(ring_place(at) - ring_place(me ^ k)) & 3 for k in range(4)]
        pieces = part.reshape(group, own, -1)
        pieces = [lax.dynamic_index_in_dim(pieces, place, 0, keepdims=False) for place in places]
        summed = jnp.stack([pieces[0], pieces[2]]) + both_ways(jnp.stack([pieces[1], pieces[3]]), "sub")
        last_other = both_ways(last_over, "sub")
        other_cols = jnp.concatenate(
            [
                spread(pair, pair_over, pair_other, 0),
                spread(third, third_over, third_other, 1),
                spread(last, last_over, last_other, 1),
            ]
        )
        given = both_ways(summed[1], "feat")
        tile = covariance_of(gathered, other_cols)
        mine, given, tile = lax.optimization_barrier((summed[0], given, tile))
        total = mine + given
    else:
        total = lax.psum_scatter(part, WIDE, scatter_dimension=0, tiled=True)
        tile = covariance_of(gathered, other_cols)
    scores = jnp.transpose(total) / jnp.sqrt(jnp.float32(gathered.shape[1] * group))
    return (tile, scores)


def solution(mesh):
    placed = (
        P(("groups", "dp"), ("feat", "sub")),
        P(("groups", "dp"), ("feat", "sub")),
        P(("feat", "sub"), None),
        P(("feat", "sub"), None),
        P(("groups", "dp"), None),
        P(("groups", "dp")),
    )
    return jax.shard_map(
        shards,
        mesh=mesh,
        in_specs=placed,
        out_specs=(P(("groups", "feat", "sub"), "dp"), P(("groups", "dp"), ("feat", "sub"))),
        check_vma=False,
    )
```

```python
import jax
import jax.numpy as jnp
from jax import lax
from jax.experimental import pallas as pl
from jax.experimental.pallas import tpu as pltpu
from jax.sharding import PartitionSpec as P

F32, BF16, I32 = jnp.float32, jnp.bfloat16, jnp.int32
WIDE = ("feat", "sub")
MIB = 1 << 20
VMEM = pl.BlockSpec(memory_space=pltpu.VMEM)
SMEM = pl.BlockSpec(memory_space=pltpu.SMEM)


def params(mib):
    return pltpu.CompilerParams(vmem_limit_bytes=mib * MIB)


def project_kernel(x_ref, weight_ref, full_ref):
    tile = 256
    for i in range(x_ref.shape[0] // tile):
        at = slice(i * tile, (i + 1) * tile)
        product = jnp.dot(x_ref[at, :], weight_ref[...], preferred_element_type=F32)
        full_ref[:, at] = jnp.transpose(product)


def project_flipped_kernel(x_ref, weight_ref, full_ref, flip_ref):
    flip_ref[...] = jnp.transpose(weight_ref[...])
    project_kernel(x_ref, flip_ref, full_ref)


def project(x, weight, flipped):
    rows, width = x.shape
    rank = weight.shape[0] if flipped else weight.shape[1]
    return pl.pallas_call(
        project_flipped_kernel if flipped else project_kernel,
        in_specs=[VMEM, VMEM],
        out_specs=VMEM,
        out_shape=jax.ShapeDtypeStruct((rank, rows), F32),
        scratch_shapes=[pltpu.VMEM((width, rank), BF16)] if flipped else [],
        compiler_params=params(16),
        cost_estimate=pl.CostEstimate(
            flops=(40 if flipped else 2) * rows * width * rank, bytes_accessed=2 * x.size, transcendentals=0
        ),
        name="project",
    )(x, weight)


def split(x):
    high = x.astype(BF16)
    return high, (x - high.astype(F32)).astype(BF16)


def feature_kernel(start_ref, end_ref, u_ref, v_ref, scale_ref, feat_ref, uu, vh, vl, acc, wide):
    rank_in = u_ref.shape[0]
    share = v_ref.shape[0]
    tokens = u_ref.shape[1]
    seqs = scale_ref.shape[0]
    tile = 256
    high, low = split(u_ref[...])
    uu[:tokens, :] = jnp.transpose(jnp.concatenate([high, low], axis=0))
    uu[tokens:, :] = jnp.zeros((uu.shape[0] - tokens, uu.shape[1]), BF16)
    high, low = split(v_ref[...])
    vh[:, :tokens] = high
    vl[:, :tokens] = low
    for ref in (vh, vl):
        ref[:, tokens:] = jnp.zeros((ref.shape[0], ref.shape[1] - tokens), BF16)
    lane = lax.broadcasted_iota(I32, (8, tile), 1)
    left = lax.broadcasted_iota(I32, (8, 2 * rank_in), 1) < rank_in
    for group in range(seqs // 8):
        sets = (8 * group, 8 * group + 4)
        bases = [(start_ref[s] // 128) * 128 for s in sets]
        needs = [(end_ref[s + 3] - base + tile - 1) // tile for s, base in zip(sets, bases)]
        acc[...] = jnp.zeros_like(acc)

        def step(k, carry):
            for i in range(2):
                at = pl.multiple_of(bases[i] + k * tile, 128)
                tops, lows = [], []
                v_high = vh[:, pl.ds(at, tile)]
                v_low = vl[:, pl.ds(at, tile)]
                for s in range(sets[i], sets[i] + 4):
                    begin = start_ref[s] - at
                    stop = end_ref[s] - at
                    inside = jnp.where((lane >= begin) & (lane < stop), 1.0, 0.0).astype(F32)
                    inside = jnp.concatenate([inside] * (share // 8), axis=0).astype(BF16)
                    tops.append(v_high * inside)
                    lows.append(v_low * inside)
                total = jnp.dot(
                    jnp.concatenate(tops + lows, 0),
                    uu[pl.ds(at, tile), :],
                    preferred_element_type=F32,
                )
                rows = slice(4 * share * i, 4 * share * (i + 1))
                acc[rows, :] += total[: 4 * share] + total[4 * share :]
            return carry

        lax.fori_loop(0, jnp.maximum(needs[0], needs[1]), step, 0)
        factor = scale_ref[8 * group : 8 * group + 8, :]
        for pair in range(share // 2):
            even = acc[pl.ds(2 * pair, 8, stride=share), :]
            odd = acc[pl.ds(2 * pair + 1, 8, stride=share), :]
            even = even + pltpu.roll(even, rank_in, 1)
            odd = odd + pltpu.roll(odd, rank_in, 1)
            both = jnp.where(left, even, odd) * factor
            wide[8 * group : 8 * group + 8, 2 * rank_in * pair : 2 * rank_in * (pair + 1)] = both
    feat_ref[...] = wide[...].astype(BF16)


def features_of(starts, ends, u, v, scale):
    rank_in, tokens = u.shape
    share = v.shape[0]
    seqs = starts.shape[0]
    return pl.pallas_call(
        feature_kernel,
        in_specs=[SMEM, SMEM, VMEM, VMEM, VMEM],
        out_specs=VMEM,
        out_shape=jax.ShapeDtypeStruct((seqs, share * rank_in), BF16),
        scratch_shapes=[
            pltpu.VMEM((tokens + 768, 2 * rank_in), BF16),
            pltpu.VMEM((share, tokens + 768), BF16),
            pltpu.VMEM((share, tokens + 768), BF16),
            pltpu.VMEM((8 * share, 2 * rank_in), F32),
            pltpu.VMEM((seqs, share * rank_in), F32),
        ],
        compiler_params=params(16),
        name="features",
    )(starts, ends, u, v, scale)


def score_kernel(ids_ref, all_ref, square_ref, part_ref):
    every = all_ref[...]
    seqs = every.shape[0]
    picks = ids_ref.shape[0]
    weights = 1.0 / (square_ref[...] / seqs + 1e-05)
    column = lax.broadcasted_iota(I32, (picks, seqs), 1)
    chosen_of = jnp.where(column == ids_ref[...], 1.0, 0.0).astype(BF16)
    chosen = jnp.dot(chosen_of, every, preferred_element_type=F32)
    weighted = (chosen * weights).astype(BF16)
    part_ref[...] = lax.dot_general(
        every, weighted, (((1,), (1,)), ((), ())), preferred_element_type=F32
    )


def partial_scores_of(ids, gathered, squares):
    return pl.pallas_call(
        score_kernel,
        in_specs=[VMEM, VMEM, VMEM],
        out_specs=VMEM,
        out_shape=jax.ShapeDtypeStruct((gathered.shape[0], ids.shape[0]), F32),
        compiler_params=params(24),
        cost_estimate=pl.CostEstimate(flops=8 * gathered.size * ids.shape[0], bytes_accessed=2 * gathered.size, transcendentals=0),
        name="partial_scores",
    )(ids[:, None], gathered, squares)


def covariance_kernel(row_ref, col_ref, one_ref, two_ref, tile_hbm, score_hbm, tile_ref, score_ref, sem):
    seqs = row_ref.shape[0]
    steps = sem.shape[0] - 1
    tile = tile_ref.shape[0] // steps
    score_ref[...] = one_ref[...] + two_ref[...]
    copies = [pltpu.make_async_copy(score_ref, score_hbm, sem.at[steps])]
    copies[0].start()
    for i in range(steps):
        at = slice(i * tile, (i + 1) * tile)
        product = lax.dot_general(
            row_ref[:, at], col_ref[...], (((0,), (0,)), ((), ())), preferred_element_type=F32
        )
        tile_ref[at, :] = product * (1.0 / seqs)
        rows = pl.ds(i * tile, tile)
        copies.append(pltpu.make_async_copy(tile_ref.at[rows], tile_hbm.at[rows], sem.at[i]))
        copies[-1].start()
    for copy in copies:
        copy.wait()


def covariance_of(gathered, other_cols, one, two):
    seqs, rows = gathered.shape
    cols = other_cols.shape[1]
    steps = rows // 256
    return pl.pallas_call(
        covariance_kernel,
        in_specs=[VMEM] * 4,
        out_specs=[pl.BlockSpec(memory_space=pltpu.HBM)] * 2,
        out_shape=[jax.ShapeDtypeStruct((rows, cols), F32), jax.ShapeDtypeStruct(one.shape, F32)],
        scratch_shapes=[
            pltpu.VMEM((rows, cols), F32),
            pltpu.VMEM(one.shape, F32),
            pltpu.SemaphoreType.DMA((steps + 1,)),
        ],
        compiler_params=params(32),
        cost_estimate=pl.CostEstimate(flops=2 * seqs * rows * cols, bytes_accessed=4 * rows * cols, transcendentals=0),
        name="covariance",
    )(gathered, other_cols, one, two)


def both_ways(x, axis):
    return lax.ppermute(x, axis, [(0, 1), (1, 0)])


def picked(index, low, high):
    return jnp.where(index == 0, low, high)


STEPS = 32000.0


def coded(give):
    top = jnp.max(jnp.abs(give), axis=1, keepdims=True)
    power = jnp.ceil(jnp.log2(jnp.maximum(top, 1e-30)))
    steps = jnp.round(give * (jnp.exp2(-power) * STEPS))
    both = jnp.concatenate([steps, jnp.broadcast_to(power, (give.shape[0], 128))], axis=1)
    return both.astype(jnp.int16)


def decoded(got):
    got = got.astype(F32)
    return got[:, :-128] * (jnp.exp2(got[:, -128:-127]) * (1.0 / STEPS))


def u_of_chip(u):
    half = u.shape[0] // 2
    sub = lax.axis_index("sub")
    return picked(sub, u[:half], u[half:]) + both_ways(picked(sub, u[half:], u[:half]), "sub")


def reduced(u_chip, v, share):
    feat, sub = lax.axis_index("feat"), lax.axis_index("sub")
    u_got = both_ways(coded(u_chip), "feat")
    v = v.reshape(2, 2, share, -1)
    v_chip = picked(sub, v[:, 0], v[:, 1]) + both_ways(picked(sub, v[:, 1], v[:, 0]), "sub")
    v_given = coded(picked(feat, v_chip[1], v_chip[0]))
    u_got = lax.optimization_barrier((u_got, v_given))[0]
    v_got = both_ways(v_given, "feat")
    u_mine = u_chip + decoded(u_got)
    u_other = both_ways(u_mine, "sub")
    u = jnp.concatenate([picked(sub, u_mine, u_other), picked(sub, u_other, u_mine)])
    return u, picked(feat, v_chip[0], v_chip[1]) + decoded(v_got)


def is_square():
    return lax.axis_size("feat") == 2 and lax.axis_size("sub") == 2 and lax.axis_size("dp") == 4


RING = (0, 1, 3, 2)


def ring_place(d):
    return d ^ (d >> 1)


def around(part):
    return lax.ppermute(part, "dp", [(RING[i], RING[(i + 1) % 4]) for i in range(4)])


def on_owner_chip():
    return (lax.axis_index(WIDE) ^ lax.axis_index("dp")) < 2


def owned(part, other):
    return jnp.where(lax.axis_index(WIDE) == lax.axis_index("dp"), part, other)


def sent_across(part):
    size = part.shape[1] // 2
    half = picked(lax.axis_index("sub"), part[:, :size], part[:, size:])
    return both_ways(half, "feat")


def spread(part, mine, other):
    sub = lax.axis_index("sub")
    both = jnp.concatenate([picked(sub, mine, other), picked(sub, other, mine)], axis=1)
    return jnp.where(on_owner_chip(), part, both)


def summed_squares(part):
    return jnp.sum(jnp.square(part.astype(F32)), axis=0, keepdims=True)


def column_block(gathered, col_width):
    block_width = gathered.shape[1]
    col_start = lax.axis_index("dp") * col_width
    owner = col_start // block_width
    own_slice = lax.dynamic_slice_in_dim(gathered, col_start % block_width, col_width, 1)
    every_slice = lax.all_gather(own_slice, WIDE, axis=1, tiled=True)
    return lax.dynamic_slice_in_dim(every_slice, owner * col_width, col_width, 1)


def shards(layer_inputs, output_grads, proj_in, proj_out, lengths, target_ids):
    group = lax.axis_size(WIDE)
    rank_in = proj_in.shape[1]
    share = proj_out.shape[1] // group
    u = project(layer_inputs, jnp.transpose(proj_in), True)
    if is_square():
        u_chip = u_of_chip(u)
        v = project(output_grads, proj_out, False)
        u, v_mine = reduced(u_chip, v, share)
    else:
        v = project(output_grads, proj_out, False)
        u = lax.psum(u, WIDE)
        v_mine = lax.psum_scatter(v, WIDE, scatter_dimension=0, tiled=True)
    seq_len = lengths[0]
    ends = jnp.cumsum(seq_len)
    starts = ends - seq_len
    scale = jnp.broadcast_to(1.0 / jnp.sqrt(seq_len.astype(F32))[:, None], (seq_len.shape[0], 2 * rank_in))
    local_feat = features_of(starts, ends, u, v_mine, scale)
    me = lax.axis_index(WIDE)
    at = lax.axis_index("dp")
    if is_square():
        chunks, owns, overs = [local_feat], [], []
        for k in range(3):
            chunks.append(around(chunks[k]))
            owns.append(owned(chunks[k], both_ways(chunks[k], "sub")))
            overs.append(sent_across(owns[k]))
            chunks[k + 1], overs[k] = lax.optimization_barrier((chunks[k + 1], overs[k]))
        last = owned(chunks[3], both_ways(chunks[3], "sub"))
        early_over = jnp.concatenate(overs)
        early_other = both_ways(early_over, "sub")
        gathered = jnp.concatenate(chunks)
        squares = summed_squares(gathered)
        seqs = local_feat.shape[0]
        ids = ((ring_place(at) - ring_place(target_ids // seqs)) & 3) * seqs + target_ids % seqs
    else:
        gathered = lax.all_gather(local_feat, "dp", axis=0, tiled=True)
        other_cols = column_block(gathered, gathered.shape[1] * group // lax.axis_size("dp"))
        ids = target_ids
        squares = summed_squares(gathered)
    part = partial_scores_of(ids, gathered, squares) / jnp.sqrt(jnp.float32(gathered.shape[1] * group))
    if is_square():
        last, part = lax.optimization_barrier((last, part))
        last_over = sent_across(last)
    own = part.shape[0] // group
    if is_square():
        places = [(ring_place(at) - ring_place(me ^ k)) & 3 for k in range(4)]
        pieces = part.reshape(group, own, -1)
        pieces = [lax.dynamic_index_in_dim(pieces, place, 0, keepdims=False) for place in places]
        summed = jnp.stack([pieces[0], pieces[2]]) + both_ways(jnp.stack([pieces[1], pieces[3]]), "sub")
        last_other = both_ways(last_over, "sub")
        early = spread(jnp.concatenate(owns), early_over, early_other)
        other_cols = jnp.concatenate([early, spread(last, last_over, last_other)])
        mine, given = summed[0], both_ways(summed[1], "feat")
    else:
        mine, given = lax.psum_scatter(part, WIDE, scatter_dimension=0, tiled=True), jnp.zeros((own, ids.shape[0]), F32)
    tile, total = covariance_of(gathered, other_cols, mine, given)
    return (tile, jnp.transpose(total))


def solution(mesh):
    placed = (
        P(("groups", "dp"), ("feat", "sub")),
        P(("groups", "dp"), ("feat", "sub")),
        P(("feat", "sub"), None),
        P(("feat", "sub"), None),
        P(("groups", "dp"), None),
        P(("groups", "dp")),
    )
    return jax.shard_map(
        shards,
        mesh=mesh,
        in_specs=placed,
        out_specs=(P(("groups", "feat", "sub"), "dp"), P(("groups", "dp"), ("feat", "sub"))),
        check_vma=False,
    )
```

```python
import functools

import jax
import jax.numpy as jnp
from jax import lax
from jax.experimental import pallas as pl
from jax.experimental.pallas import tpu as pltpu
from jax.sharding import PartitionSpec as P

F32, BF16, I32 = jnp.float32, jnp.bfloat16, jnp.int32
WIDE = ("feat", "sub")
MIB = 1 << 20
VMEM = pl.BlockSpec(memory_space=pltpu.VMEM)
SMEM = pl.BlockSpec(memory_space=pltpu.SMEM)


def params(mib):
    return pltpu.CompilerParams(vmem_limit_bytes=mib * MIB)


def project_kernel(x_ref, weight_ref, full_ref):
    tile = 256
    for i in range(x_ref.shape[0] // tile):
        at = slice(i * tile, (i + 1) * tile)
        product = jnp.dot(x_ref[at, :], weight_ref[...], preferred_element_type=F32)
        full_ref[:, at] = jnp.transpose(product)


def project_flipped_kernel(x_ref, weight_ref, full_ref, flip_ref):
    flip_ref[...] = jnp.transpose(weight_ref[...])
    project_kernel(x_ref, flip_ref, full_ref)


def project(x, weight, flipped):
    rows, width = x.shape
    rank = weight.shape[0] if flipped else weight.shape[1]
    return pl.pallas_call(
        project_flipped_kernel if flipped else project_kernel,
        in_specs=[VMEM, VMEM],
        out_specs=VMEM,
        out_shape=jax.ShapeDtypeStruct((rank, rows), F32),
        scratch_shapes=[pltpu.VMEM((width, rank), BF16)] if flipped else [],
        compiler_params=params(16),
        cost_estimate=pl.CostEstimate(
            flops=(40 if flipped else 2) * rows * width * rank, bytes_accessed=2 * x.size, transcendentals=0
        ),
        name="project",
    )(x, weight)


def split(x):
    high = x.astype(BF16)
    return high, (x - high.astype(F32)).astype(BF16)


def feature_kernel(start_ref, end_ref, u_ref, v_ref, scale_ref, feat_ref, uu, vh, vl, acc, wide):
    rank_in = u_ref.shape[0]
    share = v_ref.shape[0]
    tokens = u_ref.shape[1]
    seqs = scale_ref.shape[0]
    tile = 256
    high, low = split(u_ref[...])
    uu[:tokens, :] = jnp.transpose(jnp.concatenate([high, low], axis=0))
    uu[tokens:, :] = jnp.zeros((uu.shape[0] - tokens, uu.shape[1]), BF16)
    high, low = split(v_ref[...])
    vh[:, :tokens] = high
    vl[:, :tokens] = low
    for ref in (vh, vl):
        ref[:, tokens:] = jnp.zeros((ref.shape[0], ref.shape[1] - tokens), BF16)
    lane = lax.broadcasted_iota(I32, (8, tile), 1)
    left = lax.broadcasted_iota(I32, (8, 2 * rank_in), 1) < rank_in
    sets = range(0, seqs, 4)
    bases = [(start_ref[s] // 128) * 128 for s in sets]
    needs = [(end_ref[s + 3] - base + tile - 1) // tile for s, base in zip(sets, bases)]

    def add(k, begun):
        for i, first in enumerate(sets):
            at = pl.multiple_of(bases[i] + k * tile, 128)
            tops, lows = [], []
            v_high = vh[:, pl.ds(at, tile)]
            v_low = vl[:, pl.ds(at, tile)]
            for s in range(first, first + 4):
                begin = start_ref[s] - at
                stop = end_ref[s] - at
                inside = jnp.where((lane >= begin) & (lane < stop), 1.0, 0.0).astype(F32)
                inside = jnp.concatenate([inside] * (share // 8), axis=0).astype(BF16)
                tops.append(v_high * inside)
                lows.append(v_low * inside)
            total = jnp.dot(
                jnp.concatenate(tops + lows, 0), uu[pl.ds(at, tile), :], preferred_element_type=F32
            )
            total = total[: 4 * share] + total[4 * share :]
            rows = slice(4 * share * i, 4 * share * (i + 1))
            acc[rows, :] = acc[rows, :] + total if begun else total

    add(0, False)
    lax.fori_loop(1, functools.reduce(jnp.maximum, needs), lambda k, carry: add(k, True) or carry, 0)
    for group in range(seqs // 8):
        factor = scale_ref[8 * group : 8 * group + 8, :]
        for pair in range(share // 2):
            row = 8 * share * group + 2 * pair
            even = acc[pl.ds(row, 8, stride=share), :]
            odd = acc[pl.ds(row + 1, 8, stride=share), :]
            even = even + pltpu.roll(even, rank_in, 1)
            odd = odd + pltpu.roll(odd, rank_in, 1)
            both = jnp.where(left, even, odd) * factor
            wide[8 * group : 8 * group + 8, 2 * rank_in * pair : 2 * rank_in * (pair + 1)] = both
    feat_ref[...] = wide[...].astype(BF16)


def features_of(starts, ends, u, v, scale):
    rank_in, tokens = u.shape
    share = v.shape[0]
    seqs = starts.shape[0]
    return pl.pallas_call(
        feature_kernel,
        in_specs=[SMEM, SMEM, VMEM, VMEM, VMEM],
        out_specs=VMEM,
        out_shape=jax.ShapeDtypeStruct((seqs, share * rank_in), BF16),
        scratch_shapes=[
            pltpu.VMEM((tokens + 768, 2 * rank_in), BF16),
            pltpu.VMEM((share, tokens + 768), BF16),
            pltpu.VMEM((share, tokens + 768), BF16),
            pltpu.VMEM((seqs * share, 2 * rank_in), F32),
            pltpu.VMEM((seqs, share * rank_in), F32),
        ],
        compiler_params=params(16),
        name="features",
    )(starts, ends, u, v, scale)


def score_kernel(ids_ref, all_ref, square_ref, part_ref):
    every = all_ref[...]
    seqs = every.shape[0]
    picks = ids_ref.shape[0]
    weights = 1.0 / (square_ref[...] / seqs + 1e-05)
    column = lax.broadcasted_iota(I32, (picks, seqs), 1)
    chosen_of = jnp.where(column == ids_ref[...], 1.0, 0.0).astype(BF16)
    chosen = jnp.dot(chosen_of, every, preferred_element_type=F32)
    weighted = (chosen * weights).astype(BF16)
    part_ref[...] = lax.dot_general(
        every, weighted, (((1,), (1,)), ((), ())), preferred_element_type=F32
    )


def partial_scores_of(ids, gathered, squares):
    return pl.pallas_call(
        score_kernel,
        in_specs=[VMEM, VMEM, VMEM],
        out_specs=VMEM,
        out_shape=jax.ShapeDtypeStruct((gathered.shape[0], ids.shape[0]), F32),
        compiler_params=params(24),
        cost_estimate=pl.CostEstimate(flops=8 * gathered.size * ids.shape[0], bytes_accessed=2 * gathered.size, transcendentals=0),
        name="partial_scores",
    )(ids[:, None], gathered, squares)


def covariance_kernel(row_ref, col_ref, one_ref, two_ref, tile_hbm, score_hbm, tile_ref, score_ref, sem):
    seqs = row_ref.shape[0]
    steps = sem.shape[0] - 1
    tile = tile_ref.shape[0] // steps
    score_ref[...] = one_ref[...] + two_ref[...]
    copies = [pltpu.make_async_copy(score_ref, score_hbm, sem.at[steps])]
    copies[0].start()
    for i in range(steps):
        at = slice(i * tile, (i + 1) * tile)
        product = lax.dot_general(
            row_ref[:, at], col_ref[...], (((0,), (0,)), ((), ())), preferred_element_type=F32
        )
        tile_ref[at, :] = product * (1.0 / seqs)
        rows = pl.ds(i * tile, tile)
        copies.append(pltpu.make_async_copy(tile_ref.at[rows], tile_hbm.at[rows], sem.at[i]))
        copies[-1].start()
    for copy in copies:
        copy.wait()


def covariance_of(gathered, other_cols, one, two):
    seqs, rows = gathered.shape
    cols = other_cols.shape[1]
    steps = rows // 256
    return pl.pallas_call(
        covariance_kernel,
        in_specs=[VMEM] * 4,
        out_specs=[pl.BlockSpec(memory_space=pltpu.HBM)] * 2,
        out_shape=[jax.ShapeDtypeStruct((rows, cols), F32), jax.ShapeDtypeStruct(one.shape, F32)],
        scratch_shapes=[
            pltpu.VMEM((rows, cols), F32),
            pltpu.VMEM(one.shape, F32),
            pltpu.SemaphoreType.DMA((steps + 1,)),
        ],
        compiler_params=params(32),
        cost_estimate=pl.CostEstimate(flops=2 * seqs * rows * cols, bytes_accessed=4 * rows * cols, transcendentals=0),
        name="covariance",
    )(gathered, other_cols, one, two)


def both_ways(x, axis):
    return lax.ppermute(x, axis, [(0, 1), (1, 0)])


def picked(index, low, high):
    return jnp.where(index == 0, low, high)


STEPS = 32000.0


def coded(give):
    top = jnp.max(jnp.abs(give), axis=1, keepdims=True)
    power = jnp.ceil(jnp.log2(jnp.maximum(top, 1e-30)))
    steps = jnp.round(give * (jnp.exp2(-power) * STEPS))
    both = jnp.concatenate([steps, jnp.broadcast_to(power, (give.shape[0], 128))], axis=1)
    return both.astype(jnp.int16)


def decoded(got):
    got = got.astype(F32)
    return got[:, :-128] * (jnp.exp2(got[:, -128:-127]) * (1.0 / STEPS))


def u_of_chip(u):
    half = u.shape[0] // 2
    sub = lax.axis_index("sub")
    return picked(sub, u[:half], u[half:]) + both_ways(picked(sub, u[half:], u[:half]), "sub")


def reduced(u_chip, v, share):
    feat, sub = lax.axis_index("feat"), lax.axis_index("sub")
    u_got = both_ways(coded(u_chip), "feat")
    v = v.reshape(2, 2, share, -1)
    v_chip = picked(sub, v[:, 0], v[:, 1]) + both_ways(picked(sub, v[:, 1], v[:, 0]), "sub")
    v_given = coded(picked(feat, v_chip[1], v_chip[0]))
    u_got = lax.optimization_barrier((u_got, v_given))[0]
    v_got = both_ways(v_given, "feat")
    u_mine = u_chip + decoded(u_got)
    u_other = both_ways(u_mine, "sub")
    u = jnp.concatenate([picked(sub, u_mine, u_other), picked(sub, u_other, u_mine)])
    return u, picked(feat, v_chip[0], v_chip[1]) + decoded(v_got)


def is_square():
    return lax.axis_size("feat") == 2 and lax.axis_size("sub") == 2 and lax.axis_size("dp") == 4


RING = (0, 1, 3, 2)


def ring_place(d):
    return d ^ (d >> 1)


def around(part):
    return lax.ppermute(part, "dp", [(RING[i], RING[(i + 1) % 4]) for i in range(4)])


def on_owner_chip():
    return (lax.axis_index(WIDE) ^ lax.axis_index("dp")) < 2


def owned(part, other):
    return jnp.where(lax.axis_index(WIDE) == lax.axis_index("dp"), part, other)


def sent_across(part):
    size = part.shape[1] // 2
    half = picked(lax.axis_index("sub"), part[:, :size], part[:, size:])
    return both_ways(half, "feat")


def spread(part, mine, other):
    sub = lax.axis_index("sub")
    both = jnp.concatenate([picked(sub, mine, other), picked(sub, other, mine)], axis=1)
    return jnp.where(on_owner_chip(), part, both)


def summed_squares(part):
    return jnp.sum(jnp.square(part.astype(F32)), axis=0, keepdims=True)


def column_block(gathered, col_width):
    block_width = gathered.shape[1]
    col_start = lax.axis_index("dp") * col_width
    owner = col_start // block_width
    own_slice = lax.dynamic_slice_in_dim(gathered, col_start % block_width, col_width, 1)
    every_slice = lax.all_gather(own_slice, WIDE, axis=1, tiled=True)
    return lax.dynamic_slice_in_dim(every_slice, owner * col_width, col_width, 1)


def shards(layer_inputs, output_grads, proj_in, proj_out, lengths, target_ids):
    group = lax.axis_size(WIDE)
    rank_in = proj_in.shape[1]
    share = proj_out.shape[1] // group
    u = project(layer_inputs, jnp.transpose(proj_in), True)
    if is_square():
        u_chip = u_of_chip(u)
        v = project(output_grads, proj_out, False)
        u, v_mine = reduced(u_chip, v, share)
    else:
        v = project(output_grads, proj_out, False)
        u = lax.psum(u, WIDE)
        v_mine = lax.psum_scatter(v, WIDE, scatter_dimension=0, tiled=True)
    seq_len = lengths[0]
    ends = jnp.cumsum(seq_len)
    starts = ends - seq_len
    scale = jnp.broadcast_to(1.0 / jnp.sqrt(seq_len.astype(F32))[:, None], (seq_len.shape[0], 2 * rank_in))
    local_feat = features_of(starts, ends, u, v_mine, scale)
    me = lax.axis_index(WIDE)
    at = lax.axis_index("dp")
    if is_square():
        chunks, owns, overs = [local_feat], [], []
        for k in range(3):
            chunks.append(around(chunks[k]))
            owns.append(owned(chunks[k], both_ways(chunks[k], "sub")))
            overs.append(sent_across(owns[k]))
            chunks[k + 1], overs[k] = lax.optimization_barrier((chunks[k + 1], overs[k]))
        last = owned(chunks[3], both_ways(chunks[3], "sub"))
        early_over = jnp.concatenate(overs)
        early_other = both_ways(early_over, "sub")
        gathered = jnp.concatenate(chunks)
        squares = summed_squares(gathered)
        seqs = local_feat.shape[0]
        ids = ((ring_place(at) - ring_place(target_ids // seqs)) & 3) * seqs + target_ids % seqs
    else:
        gathered = lax.all_gather(local_feat, "dp", axis=0, tiled=True)
        other_cols = column_block(gathered, gathered.shape[1] * group // lax.axis_size("dp"))
        ids = target_ids
        squares = summed_squares(gathered)
    part = partial_scores_of(ids, gathered, squares) / jnp.sqrt(jnp.float32(gathered.shape[1] * group))
    if is_square():
        last, part = lax.optimization_barrier((last, part))
        last_over = sent_across(last)
    own = part.shape[0] // group
    if is_square():
        places = [(ring_place(at) - ring_place(me ^ k)) & 3 for k in range(4)]
        pieces = part.reshape(group, own, -1)
        pieces = [lax.dynamic_index_in_dim(pieces, place, 0, keepdims=False) for place in places]
        summed = jnp.stack([pieces[0], pieces[2]]) + both_ways(jnp.stack([pieces[1], pieces[3]]), "sub")
        last_other = both_ways(last_over, "sub")
        early = spread(jnp.concatenate(owns), early_over, early_other)
        other_cols = jnp.concatenate([early, spread(last, last_over, last_other)])
        mine, given = summed[0], both_ways(summed[1], "feat")
    else:
        mine, given = lax.psum_scatter(part, WIDE, scatter_dimension=0, tiled=True), jnp.zeros((own, ids.shape[0]), F32)
    tile, total = covariance_of(gathered, other_cols, mine, given)
    return (tile, jnp.transpose(total))


def solution(mesh):
    placed = (
        P(("groups", "dp"), ("feat", "sub")),
        P(("groups", "dp"), ("feat", "sub")),
        P(("feat", "sub"), None),
        P(("feat", "sub"), None),
        P(("groups", "dp"), None),
        P(("groups", "dp")),
    )
    return jax.shard_map(
        shards,
        mesh=mesh,
        in_specs=placed,
        out_specs=(P(("groups", "feat", "sub"), "dp"), P(("groups", "dp"), ("feat", "sub"))),
        check_vma=False,
    )
```

```python
import functools

import jax
import jax.numpy as jnp
from jax import lax
from jax.experimental import pallas as pl
from jax.experimental.pallas import tpu as pltpu
from jax.sharding import PartitionSpec as P

F32, BF16, I32 = jnp.float32, jnp.bfloat16, jnp.int32
WIDE = ("feat", "sub")
MIB = 1 << 20
VMEM = pl.BlockSpec(memory_space=pltpu.VMEM)
SMEM = pl.BlockSpec(memory_space=pltpu.SMEM)


def params(mib):
    return pltpu.CompilerParams(vmem_limit_bytes=mib * MIB)


def project_kernel(x_ref, weight_ref, full_ref):
    tile = 256
    for i in range(x_ref.shape[0] // tile):
        at = slice(i * tile, (i + 1) * tile)
        product = jnp.dot(x_ref[at, :], weight_ref[...], preferred_element_type=F32)
        full_ref[:, at] = jnp.transpose(product)


def project_flipped_kernel(x_ref, weight_ref, full_ref, flip_ref):
    flip_ref[...] = jnp.transpose(weight_ref[...])
    project_kernel(x_ref, flip_ref, full_ref)


def project(x, weight, flipped):
    rows, width = x.shape
    rank = weight.shape[0] if flipped else weight.shape[1]
    return pl.pallas_call(
        project_flipped_kernel if flipped else project_kernel,
        in_specs=[VMEM, VMEM],
        out_specs=VMEM,
        out_shape=jax.ShapeDtypeStruct((rank, rows), F32),
        scratch_shapes=[pltpu.VMEM((width, rank), BF16)] if flipped else [],
        compiler_params=params(16),
        cost_estimate=pl.CostEstimate(
            flops=(40 if flipped else 2) * rows * width * rank, bytes_accessed=2 * x.size, transcendentals=0
        ),
        name="project",
    )(x, weight)


def split(x):
    high = x.astype(BF16)
    return high, (x - high.astype(F32)).astype(BF16)


def feature_kernel(start_ref, end_ref, u_ref, v_ref, scale_ref, feat_ref, uu, vh, vl, acc, wide):
    rank_in = u_ref.shape[0]
    share = v_ref.shape[0]
    tokens = u_ref.shape[1]
    seqs = scale_ref.shape[0]
    tile = 256
    high, low = split(u_ref[...])
    uu[:tokens, :] = jnp.transpose(jnp.concatenate([high, low], axis=0))
    uu[tokens:, :] = jnp.zeros((uu.shape[0] - tokens, uu.shape[1]), BF16)
    high, low = split(v_ref[...])
    vh[:, :tokens] = high
    vl[:, :tokens] = low
    for ref in (vh, vl):
        ref[:, tokens:] = jnp.zeros((ref.shape[0], ref.shape[1] - tokens), BF16)
    lane = lax.broadcasted_iota(I32, (8, tile), 1)
    left = lax.broadcasted_iota(I32, (8, 2 * rank_in), 1) < rank_in
    sets = range(0, seqs, 4)
    bases = [(start_ref[s] // 128) * 128 for s in sets]
    needs = [(end_ref[s + 3] - base + tile - 1) // tile for s, base in zip(sets, bases)]

    def add(k, begun):
        for i, first in enumerate(sets):
            at = pl.multiple_of(bases[i] + k * tile, 128)
            tops, lows = [], []
            v_high = vh[:, pl.ds(at, tile)]
            v_low = vl[:, pl.ds(at, tile)]
            for s in range(first, first + 4):
                begin = start_ref[s] - at
                stop = end_ref[s] - at
                inside = jnp.where((lane >= begin) & (lane < stop), 1.0, 0.0).astype(F32)
                inside = jnp.concatenate([inside] * (share // 8), axis=0).astype(BF16)
                tops.append(v_high * inside)
                lows.append(v_low * inside)
            total = jnp.dot(
                jnp.concatenate(tops + lows, 0), uu[pl.ds(at, tile), :], preferred_element_type=F32
            )
            total = total[: 4 * share] + total[4 * share :]
            rows = slice(4 * share * i, 4 * share * (i + 1))
            acc[rows, :] = acc[rows, :] + total if begun else total

    add(0, False)
    lax.fori_loop(1, functools.reduce(jnp.maximum, needs), lambda k, carry: add(k, True) or carry, 0)
    for group in range(seqs // 8):
        factor = scale_ref[8 * group : 8 * group + 8, :]
        for pair in range(share // 2):
            row = 8 * share * group + 2 * pair
            even = acc[pl.ds(row, 8, stride=share), :]
            odd = acc[pl.ds(row + 1, 8, stride=share), :]
            even = even + pltpu.roll(even, rank_in, 1)
            odd = odd + pltpu.roll(odd, rank_in, 1)
            both = jnp.where(left, even, odd) * factor
            wide[8 * group : 8 * group + 8, 2 * rank_in * pair : 2 * rank_in * (pair + 1)] = both
    feat_ref[...] = wide[...].astype(BF16)


def features_of(starts, ends, u, v, scale):
    rank_in, tokens = u.shape
    share = v.shape[0]
    seqs = starts.shape[0]
    return pl.pallas_call(
        feature_kernel,
        in_specs=[SMEM, SMEM, VMEM, VMEM, VMEM],
        out_specs=VMEM,
        out_shape=jax.ShapeDtypeStruct((seqs, share * rank_in), BF16),
        scratch_shapes=[
            pltpu.VMEM((tokens + 768, 2 * rank_in), BF16),
            pltpu.VMEM((share, tokens + 768), BF16),
            pltpu.VMEM((share, tokens + 768), BF16),
            pltpu.VMEM((seqs * share, 2 * rank_in), F32),
            pltpu.VMEM((seqs, share * rank_in), F32),
        ],
        compiler_params=params(16),
        name="features",
    )(starts, ends, u, v, scale)


def score_kernel(ids_ref, all_ref, square_ref, part_ref):
    every = all_ref[...]
    seqs = every.shape[0]
    picks = ids_ref.shape[0]
    weights = 1.0 / (square_ref[...] / seqs + 1e-05)
    column = lax.broadcasted_iota(I32, (picks, seqs), 1)
    chosen_of = jnp.where(column == ids_ref[...], 1.0, 0.0).astype(BF16)
    chosen = jnp.dot(chosen_of, every, preferred_element_type=F32)
    weighted = (chosen * weights).astype(BF16)
    part_ref[...] = lax.dot_general(
        every, weighted, (((1,), (1,)), ((), ())), preferred_element_type=F32
    )


def partial_scores_of(ids, gathered, squares):
    return pl.pallas_call(
        score_kernel,
        in_specs=[VMEM, VMEM, VMEM],
        out_specs=VMEM,
        out_shape=jax.ShapeDtypeStruct((gathered.shape[0], ids.shape[0]), F32),
        compiler_params=params(24),
        cost_estimate=pl.CostEstimate(flops=8 * gathered.size * ids.shape[0], bytes_accessed=2 * gathered.size, transcendentals=0),
        name="partial_scores",
    )(ids[:, None], gathered, squares)


def covariance_kernel(row_ref, col_ref, tile_hbm, tile_ref, sem):
    seqs = row_ref.shape[0]
    steps = sem.shape[0]
    tile = tile_ref.shape[0] // steps
    copies = []
    for i in range(steps):
        at = slice(i * tile, (i + 1) * tile)
        product = lax.dot_general(
            row_ref[:, at], col_ref[...], (((0,), (0,)), ((), ())), preferred_element_type=F32
        )
        tile_ref[at, :] = product * (1.0 / seqs)
        rows = pl.ds(i * tile, tile)
        copies.append(pltpu.make_async_copy(tile_ref.at[rows], tile_hbm.at[rows], sem.at[i]))
        copies[-1].start()
    for copy in copies:
        copy.wait()


def covariance_of(gathered, other_cols):
    seqs, rows = gathered.shape
    cols = other_cols.shape[1]
    steps = rows // 256
    return pl.pallas_call(
        covariance_kernel,
        in_specs=[VMEM, VMEM],
        out_specs=pl.BlockSpec(memory_space=pltpu.HBM),
        out_shape=jax.ShapeDtypeStruct((rows, cols), F32),
        scratch_shapes=[pltpu.VMEM((rows, cols), F32), pltpu.SemaphoreType.DMA((steps,))],
        compiler_params=params(32),
        cost_estimate=pl.CostEstimate(flops=2 * seqs * rows * cols, bytes_accessed=4 * rows * cols, transcendentals=0),
        name="covariance",
    )(gathered, other_cols)


def both_ways(x, axis):
    return lax.ppermute(x, axis, [(0, 1), (1, 0)])


def picked(index, low, high):
    return jnp.where(index == 0, low, high)


STEPS = 32000.0


def coded(give):
    top = jnp.max(jnp.abs(give), axis=1, keepdims=True)
    power = jnp.ceil(jnp.log2(jnp.maximum(top, 1e-30)))
    steps = jnp.round(give * (jnp.exp2(-power) * STEPS))
    both = jnp.concatenate([steps, jnp.broadcast_to(power, (give.shape[0], 128))], axis=1)
    return both.astype(jnp.int16)


def decoded(got):
    got = got.astype(F32)
    return got[:, :-128] * (jnp.exp2(got[:, -128:-127]) * (1.0 / STEPS))


def u_of_chip(u):
    half = u.shape[0] // 2
    sub = lax.axis_index("sub")
    return picked(sub, u[:half], u[half:]) + both_ways(picked(sub, u[half:], u[:half]), "sub")


def reduced(u_chip, v, share):
    feat, sub = lax.axis_index("feat"), lax.axis_index("sub")
    u_got = both_ways(coded(u_chip), "feat")
    v = v.reshape(2, 2, share, -1)
    v_chip = picked(sub, v[:, 0], v[:, 1]) + both_ways(picked(sub, v[:, 1], v[:, 0]), "sub")
    v_given = coded(picked(feat, v_chip[1], v_chip[0]))
    u_got = lax.optimization_barrier((u_got, v_given))[0]
    v_got = both_ways(v_given, "feat")
    u_mine = u_chip + decoded(u_got)
    u_other = both_ways(u_mine, "sub")
    u = jnp.concatenate([picked(sub, u_mine, u_other), picked(sub, u_other, u_mine)])
    return u, picked(feat, v_chip[0], v_chip[1]) + decoded(v_got)


def is_square():
    return lax.axis_size("feat") == 2 and lax.axis_size("sub") == 2 and lax.axis_size("dp") == 4


RING = (0, 1, 3, 2)


def ring_place(d):
    return d ^ (d >> 1)


def around(part):
    return lax.ppermute(part, "dp", [(RING[i], RING[(i + 1) % 4]) for i in range(4)])


def against(part):
    return lax.ppermute(part, "dp", [(RING[(i + 1) % 4], RING[i]) for i in range(4)])


def on_owner_chip():
    return (lax.axis_index(WIDE) ^ lax.axis_index("dp")) < 2


def owned(part, other):
    return jnp.where(lax.axis_index(WIDE) == lax.axis_index("dp"), part, other)


def half_of(part):
    size = part.shape[1] // 2
    return picked(lax.axis_index("sub"), part[:, :size], part[:, size:])


def spread(part, mine, other):
    sub = lax.axis_index("sub")
    both = jnp.concatenate([picked(sub, mine, other), picked(sub, other, mine)], axis=1)
    return jnp.where(on_owner_chip(), part, both)


def summed_squares(part):
    return jnp.sum(jnp.square(part.astype(F32)), axis=0, keepdims=True)


def column_block(gathered, col_width):
    block_width = gathered.shape[1]
    col_start = lax.axis_index("dp") * col_width
    owner = col_start // block_width
    own_slice = lax.dynamic_slice_in_dim(gathered, col_start % block_width, col_width, 1)
    every_slice = lax.all_gather(own_slice, WIDE, axis=1, tiled=True)
    return lax.dynamic_slice_in_dim(every_slice, owner * col_width, col_width, 1)


def shards(layer_inputs, output_grads, proj_in, proj_out, lengths, target_ids):
    group = lax.axis_size(WIDE)
    rank_in = proj_in.shape[1]
    share = proj_out.shape[1] // group
    u = project(layer_inputs, jnp.transpose(proj_in), True)
    if is_square():
        u_chip = u_of_chip(u)
        v = project(output_grads, proj_out, False)
        u, v_mine = reduced(u_chip, v, share)
    else:
        v = project(output_grads, proj_out, False)
        u = lax.psum(u, WIDE)
        v_mine = lax.psum_scatter(v, WIDE, scatter_dimension=0, tiled=True)
    seq_len = lengths[0]
    ends = jnp.cumsum(seq_len)
    starts = ends - seq_len
    scale = jnp.broadcast_to(1.0 / jnp.sqrt(seq_len.astype(F32))[:, None], (seq_len.shape[0], 2 * rank_in))
    local_feat = features_of(starts, ends, u, v_mine, scale)
    me = lax.axis_index(WIDE)
    at = lax.axis_index("dp")
    if is_square():
        before = ring_place((ring_place(at) - 1) & 3)
        swapped = both_ways(local_feat, "sub")
        owns = [owned(local_feat, swapped)]
        overs = jnp.concatenate([half_of(owns[0]), half_of(jnp.where(me == before, local_feat, swapped))], axis=1)
        chunks = [local_feat, around(local_feat)]
        chunks[1], overs = lax.optimization_barrier((chunks[1], both_ways(overs, "feat")))
        width = overs.shape[1] // 2
        overs = [overs[:, :width], overs[:, width:]]
        chunks.append(around(chunks[1]))
        owns.append(owned(chunks[1], both_ways(chunks[1], "sub")))
        over = both_ways(half_of(owns[1]), "feat")
        back = against(overs[1])
        chunks[2], over = lax.optimization_barrier((chunks[2], over))
        early_over = jnp.concatenate([overs[0], over, back])
        chunks.append(around(chunks[2]))
        owns.append(owned(chunks[2], both_ways(chunks[2], "sub")))
        over = both_ways(half_of(owns[2]), "feat")
        chunks[3], over, early_other = lax.optimization_barrier((chunks[3], over, both_ways(early_over, "sub")))
        owns.append(owned(chunks[3], both_ways(chunks[3], "sub")))
        pair = 2 * local_feat.shape[0]
        other_cols = jnp.concatenate(
            [
                spread(jnp.concatenate(owns[:2]), early_over[:pair], early_other[:pair]),
                spread(owns[2], over, both_ways(over, "sub")),
                spread(owns[3], early_over[pair:], early_other[pair:]),
            ]
        )
        gathered = jnp.concatenate(chunks)
        squares = summed_squares(gathered)
        seqs = local_feat.shape[0]
        ids = ((ring_place(at) - ring_place(target_ids // seqs)) & 3) * seqs + target_ids % seqs
    else:
        gathered = lax.all_gather(local_feat, "dp", axis=0, tiled=True)
        other_cols = column_block(gathered, gathered.shape[1] * group // lax.axis_size("dp"))
        ids = target_ids
        squares = summed_squares(gathered)
    part = partial_scores_of(ids, gathered, squares) / jnp.sqrt(jnp.float32(gathered.shape[1] * group))
    own = part.shape[0] // group
    if is_square():
        places = [(ring_place(at) - ring_place(me ^ k)) & 3 for k in range(4)]
        pieces = part.reshape(group, own, -1)
        pieces = [lax.dynamic_index_in_dim(pieces, place, 0, keepdims=False) for place in places]
        summed = jnp.stack([pieces[0], pieces[2]]) + both_ways(jnp.stack([pieces[1], pieces[3]]), "sub")
        given = both_ways(summed[1], "feat")
        tile = covariance_of(gathered, other_cols)
        mine, given, tile = lax.optimization_barrier((summed[0], given, tile))
        total = mine + given
    else:
        total = lax.psum_scatter(part, WIDE, scatter_dimension=0, tiled=True)
        tile = covariance_of(gathered, other_cols)
    return (tile, jnp.transpose(total))


def solution(mesh):
    placed = (
        P(("groups", "dp"), ("feat", "sub")),
        P(("groups", "dp"), ("feat", "sub")),
        P(("feat", "sub"), None),
        P(("feat", "sub"), None),
        P(("groups", "dp"), None),
        P(("groups", "dp")),
    )
    return jax.shard_map(
        shards,
        mesh=mesh,
        in_specs=placed,
        out_specs=(P(("groups", "feat", "sub"), "dp"), P(("groups", "dp"), ("feat", "sub"))),
        check_vma=False,
    )
```

```python
import functools

import jax
import jax.numpy as jnp
from jax import lax
from jax.experimental import pallas as pl
from jax.experimental.pallas import tpu as pltpu
from jax.sharding import PartitionSpec as P

F32, BF16, I32 = jnp.float32, jnp.bfloat16, jnp.int32
WIDE = ("feat", "sub")
MIB = 1 << 20
VMEM = pl.BlockSpec(memory_space=pltpu.VMEM)
SMEM = pl.BlockSpec(memory_space=pltpu.SMEM)


def params(mib):
    return pltpu.CompilerParams(vmem_limit_bytes=mib * MIB)


def project_kernel(x_ref, weight_ref, full_ref):
    tile = 256
    for i in range(x_ref.shape[0] // tile):
        at = slice(i * tile, (i + 1) * tile)
        product = jnp.dot(x_ref[at, :], weight_ref[...], preferred_element_type=F32)
        full_ref[:, at] = jnp.transpose(product)


def project_flipped_kernel(x_ref, weight_ref, full_ref, flip_ref):
    flip_ref[...] = jnp.transpose(weight_ref[...])
    project_kernel(x_ref, flip_ref, full_ref)


def project(x, weight, flipped):
    rows, width = x.shape
    rank = weight.shape[0] if flipped else weight.shape[1]
    return pl.pallas_call(
        project_flipped_kernel if flipped else project_kernel,
        in_specs=[VMEM, VMEM],
        out_specs=VMEM,
        out_shape=jax.ShapeDtypeStruct((rank, rows), F32),
        scratch_shapes=[pltpu.VMEM((width, rank), BF16)] if flipped else [],
        compiler_params=params(16),
        cost_estimate=pl.CostEstimate(
            flops=(40 if flipped else 2) * rows * width * rank, bytes_accessed=2 * x.size, transcendentals=0
        ),
        name="project",
    )(x, weight)


def split(x):
    high = x.astype(BF16)
    return high, (x - high.astype(F32)).astype(BF16)


def feature_kernel(start_ref, end_ref, u_ref, v_ref, scale_ref, feat_ref, uu, vh, vl, acc, wide):
    rank_in = u_ref.shape[0]
    share = v_ref.shape[0]
    tokens = u_ref.shape[1]
    seqs = scale_ref.shape[0]
    tile = 256
    high, low = split(u_ref[...])
    uu[:tokens, :] = jnp.transpose(jnp.concatenate([high, low], axis=0))
    uu[tokens:, :] = jnp.zeros((uu.shape[0] - tokens, uu.shape[1]), BF16)
    high, low = split(v_ref[...])
    vh[:, :tokens] = high
    vl[:, :tokens] = low
    for ref in (vh, vl):
        ref[:, tokens:] = jnp.zeros((ref.shape[0], ref.shape[1] - tokens), BF16)
    lane = lax.broadcasted_iota(I32, (8, tile), 1)
    left = lax.broadcasted_iota(I32, (8, 2 * rank_in), 1) < rank_in
    sets = range(0, seqs, 4)
    bases = [(start_ref[s] // 128) * 128 for s in sets]
    needs = [(end_ref[s + 3] - base + tile - 1) // tile for s, base in zip(sets, bases)]

    def add(k, begun):
        for i, first in enumerate(sets):
            at = pl.multiple_of(bases[i] + k * tile, 128)
            tops, lows = [], []
            v_high = vh[:, pl.ds(at, tile)]
            v_low = vl[:, pl.ds(at, tile)]
            for s in range(first, first + 4):
                begin = start_ref[s] - at
                stop = end_ref[s] - at
                inside = jnp.where((lane >= begin) & (lane < stop), 1.0, 0.0).astype(F32)
                inside = jnp.concatenate([inside] * (share // 8), axis=0).astype(BF16)
                tops.append(v_high * inside)
                lows.append(v_low * inside)
            total = jnp.dot(
                jnp.concatenate(tops + lows, 0), uu[pl.ds(at, tile), :], preferred_element_type=F32
            )
            total = total[: 4 * share] + total[4 * share :]
            rows = slice(4 * share * i, 4 * share * (i + 1))
            acc[rows, :] = acc[rows, :] + total if begun else total

    add(0, False)
    lax.fori_loop(1, functools.reduce(jnp.maximum, needs), lambda k, carry: add(k, True) or carry, 0)
    for group in range(seqs // 8):
        factor = scale_ref[8 * group : 8 * group + 8, :]
        for pair in range(share // 2):
            row = 8 * share * group + 2 * pair
            even = acc[pl.ds(row, 8, stride=share), :]
            odd = acc[pl.ds(row + 1, 8, stride=share), :]
            even = even + pltpu.roll(even, rank_in, 1)
            odd = odd + pltpu.roll(odd, rank_in, 1)
            both = jnp.where(left, even, odd) * factor
            wide[8 * group : 8 * group + 8, 2 * rank_in * pair : 2 * rank_in * (pair + 1)] = both
    feat_ref[...] = wide[...].astype(BF16)


def features_of(starts, ends, u, v, scale):
    rank_in, tokens = u.shape
    share = v.shape[0]
    seqs = starts.shape[0]
    return pl.pallas_call(
        feature_kernel,
        in_specs=[SMEM, SMEM, VMEM, VMEM, VMEM],
        out_specs=VMEM,
        out_shape=jax.ShapeDtypeStruct((seqs, share * rank_in), BF16),
        scratch_shapes=[
            pltpu.VMEM((tokens + 768, 2 * rank_in), BF16),
            pltpu.VMEM((share, tokens + 768), BF16),
            pltpu.VMEM((share, tokens + 768), BF16),
            pltpu.VMEM((seqs * share, 2 * rank_in), F32),
            pltpu.VMEM((seqs, share * rank_in), F32),
        ],
        compiler_params=params(16),
        name="features",
    )(starts, ends, u, v, scale)


def score_kernel(ids_ref, all_ref, part_ref):
    every = all_ref[...]
    seqs = every.shape[0]
    picks = ids_ref.shape[0]
    wide = every.astype(F32)
    weights = 1.0 / (jnp.sum(wide * wide, axis=0, keepdims=True) / seqs + 1e-05)
    column = lax.broadcasted_iota(I32, (picks, seqs), 1)
    chosen_of = jnp.where(column == ids_ref[...], 1.0, 0.0).astype(BF16)
    chosen = jnp.dot(chosen_of, every, preferred_element_type=F32)
    weighted = (chosen * weights).astype(BF16)
    part_ref[...] = lax.dot_general(
        every, weighted, (((1,), (1,)), ((), ())), preferred_element_type=F32
    )


def partial_scores_of(ids, gathered):
    return pl.pallas_call(
        score_kernel,
        in_specs=[VMEM, VMEM],
        out_specs=VMEM,
        out_shape=jax.ShapeDtypeStruct((gathered.shape[0], ids.shape[0]), F32),
        compiler_params=params(24),
        cost_estimate=pl.CostEstimate(flops=8 * gathered.size * ids.shape[0], bytes_accessed=2 * gathered.size, transcendentals=0),
        name="partial_scores",
    )(ids[:, None], gathered)


def covariance_kernel(row_ref, col_ref, tile_hbm, tile_ref, sem):
    seqs = row_ref.shape[0]
    steps = sem.shape[0]
    tile = tile_ref.shape[0] // steps
    copies = []
    for i in range(steps):
        at = slice(i * tile, (i + 1) * tile)
        product = lax.dot_general(
            row_ref[:, at], col_ref[...], (((0,), (0,)), ((), ())), preferred_element_type=F32
        )
        tile_ref[at, :] = product * (1.0 / seqs)
        rows = pl.ds(i * tile, tile)
        copies.append(pltpu.make_async_copy(tile_ref.at[rows], tile_hbm.at[rows], sem.at[i]))
        copies[-1].start()
    for copy in copies:
        copy.wait()


def covariance_of(gathered, other_cols):
    seqs, rows = gathered.shape
    cols = other_cols.shape[1]
    steps = rows // 128
    return pl.pallas_call(
        covariance_kernel,
        in_specs=[VMEM, VMEM],
        out_specs=pl.BlockSpec(memory_space=pltpu.HBM),
        out_shape=jax.ShapeDtypeStruct((rows, cols), F32),
        scratch_shapes=[pltpu.VMEM((rows, cols), F32), pltpu.SemaphoreType.DMA((steps,))],
        compiler_params=params(32),
        cost_estimate=pl.CostEstimate(flops=2 * seqs * rows * cols, bytes_accessed=4 * rows * cols, transcendentals=0),
        name="covariance",
    )(gathered, other_cols)


def both_ways(x, axis):
    return lax.ppermute(x, axis, [(0, 1), (1, 0)])


def picked(index, low, high):
    return jnp.where(index == 0, low, high)


STEPS = 32000.0


def coded(give):
    top = jnp.max(jnp.abs(give), axis=1, keepdims=True)
    power = jnp.ceil(jnp.log2(jnp.maximum(top, 1e-30)))
    steps = jnp.round(give * (jnp.exp2(-power) * STEPS))
    both = jnp.concatenate([steps, jnp.broadcast_to(power, (give.shape[0], 128))], axis=1)
    return both.astype(jnp.int16)


def decoded(got):
    got = got.astype(F32)
    return got[:, :-128] * (jnp.exp2(got[:, -128:-127]) * (1.0 / STEPS))


def u_of_chip(u):
    half = u.shape[0] // 2
    sub = lax.axis_index("sub")
    return picked(sub, u[:half], u[half:]) + both_ways(picked(sub, u[half:], u[:half]), "sub")


def reduced(u_chip, v, share):
    feat, sub = lax.axis_index("feat"), lax.axis_index("sub")
    u_got = both_ways(coded(u_chip), "feat")
    v = v.reshape(2, 2, share, -1)
    v_chip = picked(sub, v[:, 0], v[:, 1]) + both_ways(picked(sub, v[:, 1], v[:, 0]), "sub")
    v_given = coded(picked(feat, v_chip[1], v_chip[0]))
    u_got = lax.optimization_barrier((u_got, v_given))[0]
    v_got = both_ways(v_given, "feat")
    u_mine = u_chip + decoded(u_got)
    u_other = both_ways(u_mine, "sub")
    u = jnp.concatenate([picked(sub, u_mine, u_other), picked(sub, u_other, u_mine)])
    return u, picked(feat, v_chip[0], v_chip[1]) + decoded(v_got)


def is_square():
    return lax.axis_size("feat") == 2 and lax.axis_size("sub") == 2 and lax.axis_size("dp") == 4


RING = (0, 1, 3, 2)


def ring_place(d):
    return d ^ (d >> 1)


def around(part):
    return lax.ppermute(part, "dp", [(RING[i], RING[(i + 1) % 4]) for i in range(4)])


def against(part):
    return lax.ppermute(part, "dp", [(RING[(i + 1) % 4], RING[i]) for i in range(4)])


def on_owner_chip():
    return (lax.axis_index(WIDE) ^ lax.axis_index("dp")) < 2


def owned(part, other):
    return jnp.where(lax.axis_index(WIDE) == lax.axis_index("dp"), part, other)


def half_of(part):
    size = part.shape[1] // 2
    return picked(lax.axis_index("sub"), part[:, :size], part[:, size:])


def spread(part, mine, other):
    sub = lax.axis_index("sub")
    both = jnp.concatenate([picked(sub, mine, other), picked(sub, other, mine)], axis=1)
    return jnp.where(on_owner_chip(), part, both)


def column_block(gathered, col_width):
    block_width = gathered.shape[1]
    col_start = lax.axis_index("dp") * col_width
    owner = col_start // block_width
    own_slice = lax.dynamic_slice_in_dim(gathered, col_start % block_width, col_width, 1)
    every_slice = lax.all_gather(own_slice, WIDE, axis=1, tiled=True)
    return lax.dynamic_slice_in_dim(every_slice, owner * col_width, col_width, 1)


def shards(layer_inputs, output_grads, proj_in, proj_out, lengths, target_ids):
    group = lax.axis_size(WIDE)
    rank_in = proj_in.shape[1]
    share = proj_out.shape[1] // group
    u = project(layer_inputs, jnp.transpose(proj_in), True)
    if is_square():
        u_chip = u_of_chip(u)
        v = project(output_grads, proj_out, False)
        u, v_mine = reduced(u_chip, v, share)
    else:
        v = project(output_grads, proj_out, False)
        u = lax.psum(u, WIDE)
        v_mine = lax.psum_scatter(v, WIDE, scatter_dimension=0, tiled=True)
    seq_len = lengths[0]
    ends = jnp.cumsum(seq_len)
    starts = ends - seq_len
    scale = jnp.broadcast_to(1.0 / jnp.sqrt(seq_len.astype(F32))[:, None], (seq_len.shape[0], 2 * rank_in))
    local_feat = features_of(starts, ends, u, v_mine, scale)
    me = lax.axis_index(WIDE)
    at = lax.axis_index("dp")
    if is_square():
        before = ring_place((ring_place(at) - 1) & 3)
        swapped = both_ways(local_feat, "sub")
        owns = [owned(local_feat, swapped)]
        overs = jnp.concatenate([half_of(owns[0]), half_of(jnp.where(me == before, local_feat, swapped))], axis=1)
        chunks = [local_feat, around(local_feat)]
        chunks[1], overs = lax.optimization_barrier((chunks[1], both_ways(overs, "feat")))
        width = overs.shape[1] // 2
        overs = [overs[:, :width], overs[:, width:]]
        chunks.append(around(chunks[1]))
        owns.append(owned(chunks[1], both_ways(chunks[1], "sub")))
        over = both_ways(half_of(owns[1]), "feat")
        back = against(overs[1])
        chunks[2], over = lax.optimization_barrier((chunks[2], over))
        early_over = jnp.concatenate([overs[0], over, back])
        chunks.append(around(chunks[2]))
        owns.append(owned(chunks[2], both_ways(chunks[2], "sub")))
        over = both_ways(half_of(owns[2]), "feat")
        chunks[3], over, early_other = lax.optimization_barrier((chunks[3], over, both_ways(early_over, "sub")))
        owns.append(owned(chunks[3], both_ways(chunks[3], "sub")))
        pair = 2 * local_feat.shape[0]
        other_cols = jnp.concatenate(
            [
                spread(jnp.concatenate(owns[:2]), early_over[:pair], early_other[:pair]),
                spread(owns[2], over, both_ways(over, "sub")),
                spread(owns[3], early_over[pair:], early_other[pair:]),
            ]
        )
        gathered = jnp.concatenate(chunks)
        seqs = local_feat.shape[0]
        ids = ((ring_place(at) - ring_place(target_ids // seqs)) & 3) * seqs + target_ids % seqs
    else:
        gathered = lax.all_gather(local_feat, "dp", axis=0, tiled=True)
        other_cols = column_block(gathered, gathered.shape[1] * group // lax.axis_size("dp"))
        ids = target_ids
    part = partial_scores_of(ids, gathered) / jnp.sqrt(jnp.float32(gathered.shape[1] * group))
    own = part.shape[0] // group
    if is_square():
        places = [(ring_place(at) - ring_place(me ^ k)) & 3 for k in range(4)]
        pieces = part.reshape(group, own, -1)
        pieces = [lax.dynamic_index_in_dim(pieces, place, 0, keepdims=False) for place in places]
        summed = jnp.stack([pieces[0], pieces[2]]) + both_ways(jnp.stack([pieces[1], pieces[3]]), "sub")
        given = both_ways(summed[1], "feat")
        tile = covariance_of(gathered, other_cols)
        mine, given, tile = lax.optimization_barrier((summed[0], given, tile))
        total = mine + given
    else:
        total = lax.psum_scatter(part, WIDE, scatter_dimension=0, tiled=True)
        tile = covariance_of(gathered, other_cols)
    return (tile, jnp.transpose(total))


def solution(mesh):
    placed = (
        P(("groups", "dp"), ("feat", "sub")),
        P(("groups", "dp"), ("feat", "sub")),
        P(("feat", "sub"), None),
        P(("feat", "sub"), None),
        P(("groups", "dp"), None),
        P(("groups", "dp")),
    )
    return jax.shard_map(
        shards,
        mesh=mesh,
        in_specs=placed,
        out_specs=(P(("groups", "feat", "sub"), "dp"), P(("groups", "dp"), ("feat", "sub"))),
        check_vma=False,
    )
```

```python
import functools

import jax
import jax.numpy as jnp
from jax import lax
from jax.experimental import pallas as pl
from jax.experimental.pallas import tpu as pltpu
from jax.sharding import PartitionSpec as P

F32, BF16, I32 = jnp.float32, jnp.bfloat16, jnp.int32
WIDE = ("feat", "sub")
MIB = 1 << 20
VMEM = pl.BlockSpec(memory_space=pltpu.VMEM)
SMEM = pl.BlockSpec(memory_space=pltpu.SMEM)


def params(mib):
    return pltpu.CompilerParams(vmem_limit_bytes=mib * MIB)


def project_kernel(x_ref, weight_ref, full_ref):
    tile = 256
    for i in range(x_ref.shape[0] // tile):
        at = slice(i * tile, (i + 1) * tile)
        product = jnp.dot(x_ref[at, :], weight_ref[...], preferred_element_type=F32)
        full_ref[:, at] = jnp.transpose(product)


def project_flipped_kernel(x_ref, weight_ref, full_ref, flip_ref):
    flip_ref[...] = jnp.transpose(weight_ref[...])
    project_kernel(x_ref, flip_ref, full_ref)


def project(x, weight, flipped):
    rows, width = x.shape
    rank = weight.shape[0] if flipped else weight.shape[1]
    return pl.pallas_call(
        project_flipped_kernel if flipped else project_kernel,
        in_specs=[VMEM, VMEM],
        out_specs=VMEM,
        out_shape=jax.ShapeDtypeStruct((rank, rows), F32),
        scratch_shapes=[pltpu.VMEM((width, rank), BF16)] if flipped else [],
        compiler_params=params(16),
        cost_estimate=pl.CostEstimate(
            flops=(40 if flipped else 2) * rows * width * rank, bytes_accessed=2 * x.size, transcendentals=0
        ),
        name="project",
    )(x, weight)


def split(x):
    high = x.astype(BF16)
    return high, (x - high.astype(F32)).astype(BF16)


def feature_kernel(start_ref, end_ref, u_ref, v_ref, scale_ref, feat_ref, uu, vh, vl, acc, wide):
    rank_in = u_ref.shape[0]
    share = v_ref.shape[0]
    tokens = u_ref.shape[1]
    seqs = scale_ref.shape[0]
    tile = 256
    high, low = split(u_ref[...])
    uu[:tokens, :] = jnp.transpose(jnp.concatenate([high, low], axis=0))
    uu[tokens:, :] = jnp.zeros((uu.shape[0] - tokens, uu.shape[1]), BF16)
    high, low = split(v_ref[...])
    vh[:, :tokens] = high
    vl[:, :tokens] = low
    for ref in (vh, vl):
        ref[:, tokens:] = jnp.zeros((ref.shape[0], ref.shape[1] - tokens), BF16)
    lane = lax.broadcasted_iota(I32, (8, tile), 1)
    left = lax.broadcasted_iota(I32, (8, 2 * rank_in), 1) < rank_in
    sets = range(0, seqs, 4)
    bases = [(start_ref[s] // 128) * 128 for s in sets]
    needs = [(end_ref[s + 3] - base + tile - 1) // tile for s, base in zip(sets, bases)]

    def add(k, begun):
        for i, first in enumerate(sets):
            at = pl.multiple_of(bases[i] + k * tile, 128)
            tops, lows = [], []
            v_high = vh[:, pl.ds(at, tile)]
            v_low = vl[:, pl.ds(at, tile)]
            for s in range(first, first + 4):
                begin = start_ref[s] - at
                stop = end_ref[s] - at
                inside = jnp.where((lane >= begin) & (lane < stop), 1.0, 0.0).astype(F32)
                inside = jnp.concatenate([inside] * (share // 8), axis=0).astype(BF16)
                tops.append(v_high * inside)
                lows.append(v_low * inside)
            total = jnp.dot(
                jnp.concatenate(tops + lows, 0), uu[pl.ds(at, tile), :], preferred_element_type=F32
            )
            total = total[: 4 * share] + total[4 * share :]
            rows = slice(4 * share * i, 4 * share * (i + 1))
            acc[rows, :] = acc[rows, :] + total if begun else total

    add(0, False)
    lax.fori_loop(1, functools.reduce(jnp.maximum, needs), lambda k, carry: add(k, True) or carry, 0)
    for group in range(seqs // 8):
        factor = scale_ref[8 * group : 8 * group + 8, :]
        for pair in range(share // 2):
            row = 8 * share * group + 2 * pair
            even = acc[pl.ds(row, 8, stride=share), :]
            odd = acc[pl.ds(row + 1, 8, stride=share), :]
            even = even + pltpu.roll(even, rank_in, 1)
            odd = odd + pltpu.roll(odd, rank_in, 1)
            both = jnp.where(left, even, odd) * factor
            wide[8 * group : 8 * group + 8, 2 * rank_in * pair : 2 * rank_in * (pair + 1)] = both
    feat_ref[...] = wide[...].astype(BF16)


def features_of(starts, ends, u, v, scale):
    rank_in, tokens = u.shape
    share = v.shape[0]
    seqs = starts.shape[0]
    return pl.pallas_call(
        feature_kernel,
        in_specs=[SMEM, SMEM, VMEM, VMEM, VMEM],
        out_specs=VMEM,
        out_shape=jax.ShapeDtypeStruct((seqs, share * rank_in), BF16),
        scratch_shapes=[
            pltpu.VMEM((tokens + 768, 2 * rank_in), BF16),
            pltpu.VMEM((share, tokens + 768), BF16),
            pltpu.VMEM((share, tokens + 768), BF16),
            pltpu.VMEM((seqs * share, 2 * rank_in), F32),
            pltpu.VMEM((seqs, share * rank_in), F32),
        ],
        compiler_params=params(16),
        name="features",
    )(starts, ends, u, v, scale)


def score_kernel(ids_ref, all_ref, part_ref):
    every = all_ref[...]
    seqs = every.shape[0]
    picks = ids_ref.shape[0]
    wide = every.astype(F32)
    weights = 1.0 / (jnp.sum(wide * wide, axis=0, keepdims=True) / seqs + 1e-05)
    column = lax.broadcasted_iota(I32, (picks, seqs), 1)
    chosen_of = jnp.where(column == ids_ref[...], 1.0, 0.0).astype(BF16)
    chosen = jnp.dot(chosen_of, every, preferred_element_type=F32)
    weighted = (chosen * weights).astype(BF16)
    part_ref[...] = lax.dot_general(
        every, weighted, (((1,), (1,)), ((), ())), preferred_element_type=F32
    )


def partial_scores_of(ids, gathered):
    return pl.pallas_call(
        score_kernel,
        in_specs=[VMEM, VMEM],
        out_specs=VMEM,
        out_shape=jax.ShapeDtypeStruct((gathered.shape[0], ids.shape[0]), F32),
        compiler_params=params(24),
        cost_estimate=pl.CostEstimate(flops=8 * gathered.size * ids.shape[0], bytes_accessed=2 * gathered.size, transcendentals=0),
        name="partial_scores",
    )(ids[:, None], gathered)


def covariance_kernel(row_ref, col_ref, tile_hbm, tile_ref, sem):
    seqs = row_ref.shape[0]
    steps = sem.shape[0]
    tile = tile_ref.shape[0] // steps
    copies = []
    for i in range(steps):
        at = slice(i * tile, (i + 1) * tile)
        product = lax.dot_general(
            row_ref[:, at], col_ref[...], (((0,), (0,)), ((), ())), preferred_element_type=F32
        )
        tile_ref[at, :] = product * (1.0 / seqs)
        rows = pl.ds(i * tile, tile)
        copies.append(pltpu.make_async_copy(tile_ref.at[rows], tile_hbm.at[rows], sem.at[i]))
        copies[-1].start()
    for copy in copies:
        copy.wait()


def covariance_of(gathered, other_cols):
    seqs, rows = gathered.shape
    cols = other_cols.shape[1]
    steps = rows // 128
    return pl.pallas_call(
        covariance_kernel,
        in_specs=[VMEM, VMEM],
        out_specs=pl.BlockSpec(memory_space=pltpu.HBM),
        out_shape=jax.ShapeDtypeStruct((rows, cols), F32),
        scratch_shapes=[pltpu.VMEM((rows, cols), F32), pltpu.SemaphoreType.DMA((steps,))],
        compiler_params=params(32),
        cost_estimate=pl.CostEstimate(flops=2 * seqs * rows * cols, bytes_accessed=4 * rows * cols, transcendentals=0),
        name="covariance",
    )(gathered, other_cols)


def both_ways(x, axis):
    return lax.ppermute(x, axis, [(0, 1), (1, 0)])


def picked(index, low, high):
    return jnp.where(index == 0, low, high)


STEPS = 32000.0


def coded(give):
    top = jnp.max(jnp.abs(give), axis=1, keepdims=True)
    power = jnp.ceil(jnp.log2(jnp.maximum(top, 1e-30)))
    steps = jnp.round(give * (jnp.exp2(-power) * STEPS))
    both = jnp.concatenate([steps, jnp.broadcast_to(power, (give.shape[0], 128))], axis=1)
    return both.astype(jnp.int16)


def decoded(got):
    got = got.astype(F32)
    return got[:, :-128] * (jnp.exp2(got[:, -128:-127]) * (1.0 / STEPS))


def u_of_chip(u):
    half = u.shape[0] // 2
    sub = lax.axis_index("sub")
    return picked(sub, u[:half], u[half:]) + both_ways(picked(sub, u[half:], u[:half]), "sub")


def reduced(u_chip, v, share):
    feat, sub = lax.axis_index("feat"), lax.axis_index("sub")
    u_got = both_ways(coded(u_chip), "feat")
    v = v.reshape(2, 2, share, -1)
    v_chip = picked(sub, v[:, 0], v[:, 1]) + both_ways(picked(sub, v[:, 1], v[:, 0]), "sub")
    v_given = coded(picked(feat, v_chip[1], v_chip[0]))
    u_got = lax.optimization_barrier((u_got, v_given))[0]
    v_got = both_ways(v_given, "feat")
    u_mine = u_chip + decoded(u_got)
    u_other = both_ways(u_mine, "sub")
    u = jnp.concatenate([picked(sub, u_mine, u_other), picked(sub, u_other, u_mine)])
    return u, picked(feat, v_chip[0], v_chip[1]) + decoded(v_got)


def is_square():
    return lax.axis_size("feat") == 2 and lax.axis_size("sub") == 2 and lax.axis_size("dp") == 4


RING = (0, 1, 3, 2)


def ring_place(d):
    return d ^ (d >> 1)


def around(part):
    return lax.ppermute(part, "dp", [(RING[i], RING[(i + 1) % 4]) for i in range(4)])


def against(part):
    return lax.ppermute(part, "dp", [(RING[(i + 1) % 4], RING[i]) for i in range(4)])


def on_owner_chip():
    return (lax.axis_index(WIDE) ^ lax.axis_index("dp")) < 2


def owned(part, other):
    return jnp.where(lax.axis_index(WIDE) == lax.axis_index("dp"), part, other)


def half_of(part):
    size = part.shape[1] // 2
    return picked(lax.axis_index("sub"), part[:, :size], part[:, size:])


def spread(part, mine, other):
    sub = lax.axis_index("sub")
    both = jnp.concatenate([picked(sub, mine, other), picked(sub, other, mine)], axis=1)
    return jnp.where(on_owner_chip(), part, both)


def column_block(gathered, col_width):
    block_width = gathered.shape[1]
    col_start = lax.axis_index("dp") * col_width
    owner = col_start // block_width
    own_slice = lax.dynamic_slice_in_dim(gathered, col_start % block_width, col_width, 1)
    every_slice = lax.all_gather(own_slice, WIDE, axis=1, tiled=True)
    return lax.dynamic_slice_in_dim(every_slice, owner * col_width, col_width, 1)


def shards(layer_inputs, output_grads, proj_in, proj_out, lengths, target_ids):
    group = lax.axis_size(WIDE)
    rank_in = proj_in.shape[1]
    share = proj_out.shape[1] // group
    u = project(layer_inputs, jnp.transpose(proj_in), True)
    if is_square():
        u_chip = u_of_chip(u)
        v = project(output_grads, proj_out, False)
        u, v_mine = reduced(u_chip, v, share)
    else:
        v = project(output_grads, proj_out, False)
        u = lax.psum(u, WIDE)
        v_mine = lax.psum_scatter(v, WIDE, scatter_dimension=0, tiled=True)
    seq_len = lengths[0]
    ends = jnp.cumsum(seq_len)
    starts = ends - seq_len
    scale = jnp.broadcast_to(1.0 / jnp.sqrt(seq_len.astype(F32))[:, None], (seq_len.shape[0], 2 * rank_in))
    local_feat = features_of(starts, ends, u, v_mine, scale)
    me = lax.axis_index(WIDE)
    at = lax.axis_index("dp")
    if is_square():
        before = ring_place((ring_place(at) - 1) & 3)
        swapped = both_ways(local_feat, "sub")
        owns = [owned(local_feat, swapped)]
        overs = jnp.concatenate([half_of(owns[0]), half_of(jnp.where(me == before, local_feat, swapped))], axis=1)
        chunks = [local_feat, around(local_feat)]
        chunks[1], overs = lax.optimization_barrier((chunks[1], both_ways(overs, "feat")))
        width = overs.shape[1] // 2
        overs = [overs[:, :width], overs[:, width:]]
        chunks.append(around(chunks[1]))
        owns.append(owned(chunks[1], both_ways(chunks[1], "sub")))
        over = both_ways(half_of(owns[1]), "feat")
        back = against(overs[1])
        chunks[2], over = lax.optimization_barrier((chunks[2], over))
        early_over = jnp.concatenate([overs[0], over, back])
        chunks.append(around(chunks[2]))
        owns.append(owned(chunks[2], both_ways(chunks[2], "sub")))
        over = both_ways(half_of(owns[2]), "feat")
        chunks[3], over, early_other = lax.optimization_barrier((chunks[3], over, both_ways(early_over, "sub")))
        owns.append(owned(chunks[3], both_ways(chunks[3], "sub")))
        pair = 2 * local_feat.shape[0]
        other_cols = jnp.concatenate(
            [
                spread(jnp.concatenate(owns[:2]), early_over[:pair], early_other[:pair]),
                spread(owns[2], over, both_ways(over, "sub")),
                spread(owns[3], early_over[pair:], early_other[pair:]),
            ]
        )
        gathered = jnp.concatenate(chunks)
        seqs = local_feat.shape[0]
        ids = ((ring_place(at) - ring_place(target_ids // seqs)) & 3) * seqs + target_ids % seqs
    else:
        gathered = lax.all_gather(local_feat, "dp", axis=0, tiled=True)
        other_cols = column_block(gathered, gathered.shape[1] * group // lax.axis_size("dp"))
        ids = target_ids
    part = partial_scores_of(ids, gathered) / jnp.sqrt(jnp.float32(gathered.shape[1] * group))
    own = part.shape[0] // group
    if is_square():
        places = [(ring_place(at) - ring_place(me ^ k)) & 3 for k in range(4)]
        pieces = part.reshape(group, own, -1)
        pieces = [lax.dynamic_index_in_dim(pieces, place, 0, keepdims=False) for place in places]
        given = [lax.ppermute(pieces[k], WIDE, [(i, i ^ k) for i in range(4)]) for k in (1, 2, 3)]
        tile = covariance_of(gathered, other_cols)
        mine, given, tile = lax.optimization_barrier((pieces[0], given, tile))
        total = mine + given[0] + given[1] + given[2]
    else:
        total = lax.psum_scatter(part, WIDE, scatter_dimension=0, tiled=True)
        tile = covariance_of(gathered, other_cols)
    return (tile, jnp.transpose(total))


def solution(mesh):
    placed = (
        P(("groups", "dp"), ("feat", "sub")),
        P(("groups", "dp"), ("feat", "sub")),
        P(("feat", "sub"), None),
        P(("feat", "sub"), None),
        P(("groups", "dp"), None),
        P(("groups", "dp")),
    )
    return jax.shard_map(
        shards,
        mesh=mesh,
        in_specs=placed,
        out_specs=(P(("groups", "feat", "sub"), "dp"), P(("groups", "dp"), ("feat", "sub"))),
        check_vma=False,
    )
```
